256 devices in a mesh: tile: 8 (over y, core), depth: 32 (over z, x).
Axes of the slice: x: 4, y: 4, z: 8, core: 2. Of those that a mesh axis runs over, the one named last changes fastest.
Arguments:
- volume: float32 [512, 1536, 512], P('depth', 'tile'), may hold values from 0.2 to 5
- flat_field: float32 [1536, 512], P('tile'), may hold values from 0.5 to 2
Outputs:
- corrected: float32 [512, 1536, 512], P('depth', 'tile')
The draws below stay inside these ranges and needn't reach their ends.
All inputs are finite; a program needn't handle non-finite values.
Results may differ from the reference program's by a relative error of at most 0.0003.
Values sent between devices are 32-bit elements; how exact they have to be, the bound alone decides.
No kernel may reach another device: no remote copies, remote signals or barrier semaphores. Data moves between devices by JAX's collectives and lax.ppermute only.
A program may use at most 64 MiB of HBM per device.

```python
import math
import jax
import jax.numpy as jnp
from jax import lax

W = 512
R = 192
P_SIZE = 16
RADIUS = 24
H = 1536
Z = 512


def block_scale(key, dims, split, low, top_value):
    level = 1.0
    for dim, shards_of in split:
        heights = jax.random.uniform(jax.random.fold_in(jax.random.fold_in(key, 6), dim), (shards_of,), jnp.float32, low / len(split), top_value / len(split))
        level = level * jnp.repeat(jnp.exp(heights), dims[dim] // shards_of).reshape((-1,) + (1,) * (len(dims) - 1 - dim))
    return level


def setup_inputs(seed: int = 0) -> dict:
    streams_of = jax.random.split(jax.random.key(seed), 3)
    return {
        "volume": jnp.clip(jnp.exp(math.log(5.0) - 3.218876 * jax.random.uniform(streams_of[0], (Z, H, W), jnp.float32) ** block_scale(streams_of[0], (Z, H, W), ((0, 32), (1, 8)), -0.2, 0.2)), 0.2, 5.0),
        "flat_field": jnp.clip(jnp.exp(math.log(2.0) - 1.3862944 * jax.random.uniform(streams_of[1], (H, W), jnp.float32) ** block_scale(streams_of[1], (H, W), ((0, 8),), -0.2, 0.2)), 0.5, 2.0),
    }


CLIP_LIMIT = 0.08


def blur_weights(out_count, in_count, out_start, in_start, extent, radius):
    spread = radius / 3.0
    out_index = out_start + lax.iota(jnp.int32, out_count)[:, None]
    in_index = in_start + lax.iota(jnp.int32, in_count)[None, :]
    distance = (out_index - in_index).astype(jnp.float32)
    inside = (jnp.abs(out_index - in_index) <= radius) & (in_index >= 0) & (in_index < extent)
    kernel = jnp.where(inside, jnp.exp(-distance * distance / (2.0 * spread * spread)), 0.0)
    reach = lax.iota(jnp.int32, 2 * radius + 1)[None, :] - radius
    target = out_index + reach
    valid = (target >= 0) & (target < extent)
    reach_float = reach.astype(jnp.float32)
    weights = jnp.where(valid, jnp.exp(-reach_float * reach_float / (2.0 * spread * spread)), 0.0)
    normaliser = jnp.sum(weights, axis=1, keepdims=True)
    return kernel / normaliser


def reference(volume, flat_field):
    depth_total, height, col_count = volume.shape
    slab_count = depth_total // P_SIZE
    block_count = height // R
    column_weights = blur_weights(col_count, col_count, 0, 0, col_count, RADIUS)
    row_weights = [blur_weights(R, R + 2 * RADIUS, block * R, block * R - RADIUS, height, RADIUS) for block in range(block_count)]

    def blur_slab(levelled):
        across = jnp.einsum("prc,oc->pro", levelled, column_weights, precision=lax.Precision.HIGHEST)
        padded = jnp.pad(across, ((0, 0), (RADIUS, RADIUS), (0, 0)))
        pieces = []
        for block in range(block_count):
            window = padded[:, block * R:block * R + R + 2 * RADIUS]
            pieces.append(jnp.einsum("ok,pkc->poc", row_weights[block], window, precision=lax.Precision.HIGHEST))
        return jnp.concatenate(pieces, axis=1)

    def advance(carry, inputs):
        prev_last, offset = carry
        slab, slab_index = inputs
        levelled = slab / flat_field[None]
        log_planes = jnp.log(blur_slab(levelled))
        first_ratio = jnp.where(slab_index == 0, jnp.zeros_like(prev_last),
                                jnp.clip(prev_last - log_planes[0], -CLIP_LIMIT, CLIP_LIMIT))
        inner_ratios = jnp.clip(log_planes[:-1] - log_planes[1:], -CLIP_LIMIT, CLIP_LIMIT)
        ratios = jnp.concatenate([first_ratio[None], inner_ratios], axis=0)
        attenuation = offset + jnp.cumsum(ratios, axis=0)
        return (log_planes[-1], attenuation[-1]), levelled * jnp.exp(attenuation)

    start_plane = jnp.zeros((height, col_count), jnp.float32)
    slabs = volume.reshape(slab_count, P_SIZE, height, col_count)
    indices = jnp.arange(slab_count, dtype=jnp.int32)
    _, result = lax.scan(advance, (start_plane, start_plane), (slabs, indices))
    return result.reshape(depth_total, height, col_count)
```

```python
import jax
import jax.numpy as jnp
from jax import lax
from jax.sharding import PartitionSpec as P

RADIUS = 24


CLIP_LIMIT = 0.08


def padded(cells, sides, width):
    for axis, dim in sides:
        count = lax.axis_size(axis)
        ends = count - 1
        head = lax.slice_in_dim(cells, 0, width, axis=dim)
        tail = lax.slice_in_dim(cells, cells.shape[dim] - width, cells.shape[dim], axis=dim)
        cells = jnp.concatenate(
            [
                lax.ppermute(tail, axis, [(i, (i + 1) % count) for i in range(ends)]),
                cells,
                lax.ppermute(head, axis, [((i + 1) % count, i) for i in range(ends)]),
            ],
            axis=dim,
        )
    return cells


def from_behind(value, axis, steps):
    count = lax.axis_size(axis)
    first, last = (max(0, -steps), min(count, count - steps))
    return lax.ppermute(value, axis, [(source, source + steps) for source in range(first, last)])


def carried_in(total):
    rows, cols = total.shape
    pieces = total.reshape(8, rows // 8, 4, cols // 4).transpose(0, 2, 1, 3).reshape(32, rows // 8, cols // 4)
    mine = lax.all_to_all(pieces, "depth", 0, 0, tiled=True)
    earlier = jnp.cumsum(mine, axis=0) - mine
    back = lax.all_to_all(earlier, "depth", 0, 0, tiled=True)
    return back.reshape(8, 4, rows // 8, cols // 4).transpose(0, 2, 1, 3).reshape(rows, cols)


def blur_weights(out_count, in_count, out_start, in_start, extent, radius):
    spread = radius / 3.0
    out_index = out_start + lax.iota(jnp.int32, out_count)[:, None]
    in_index = in_start + lax.iota(jnp.int32, in_count)[None, :]
    distance = (out_index - in_index).astype(jnp.float32)
    inside = (jnp.abs(out_index - in_index) <= radius) & (in_index >= 0) & (in_index < extent)
    kernel = jnp.where(inside, jnp.exp(-distance * distance / (2.0 * spread * spread)), 0.0)
    reach = lax.iota(jnp.int32, 2 * radius + 1)[None, :] - radius
    target = out_index + reach
    valid = (target >= 0) & (target < extent)
    reach_float = reach.astype(jnp.float32)
    weights = jnp.where(valid, jnp.exp(-reach_float * reach_float / (2.0 * spread * spread)), 0.0)
    normaliser = jnp.sum(weights, axis=1, keepdims=True)
    return kernel / normaliser


def clipped(values):
    return jnp.clip(values, -CLIP_LIMIT, CLIP_LIMIT)


def body(volume, flat_field):
    plane_count, row_count, col_count = volume.shape
    tile_index = lax.axis_index("tile")
    depth_index = lax.axis_index("depth")
    levelled = volume / flat_field[None]
    column_weights = blur_weights(col_count, col_count, 0, 0, col_count, RADIUS)
    across = jnp.einsum("prc,oc->pro", levelled, column_weights, precision=lax.Precision.HIGHEST)
    extended = padded(across, (("tile", 1),), RADIUS)
    row_start = tile_index * row_count
    row_weights = blur_weights(
        row_count,
        row_count + 2 * RADIUS,
        row_start,
        row_start - RADIUS,
        row_count * lax.axis_size("tile"),
        RADIUS,
    )
    blurred = jnp.einsum("ok,pkc->poc", row_weights, extended, precision=lax.Precision.HIGHEST)
    log_planes = jnp.log(blurred)
    inner_ratios = clipped(log_planes[:-1] - log_planes[1:])
    empty_plane = jnp.zeros((row_count, col_count), jnp.float32)
    prev_last = from_behind(log_planes[-1], "depth", 1)
    first_ratio = jnp.where(depth_index == 0, empty_plane, clipped(prev_last - log_planes[0]))
    local_sums = jnp.cumsum(jnp.concatenate([first_ratio[None], inner_ratios], axis=0), axis=0)

    offset = carried_in(local_sums[-1])
    attenuation = local_sums + offset[None]
    return levelled * jnp.exp(attenuation)


def solution(mesh):
    return jax.shard_map(
        body,
        mesh=mesh,
        in_specs=(P("depth", "tile", None), P("tile", None)),
        out_specs=P("depth", "tile", None),
        check_vma=False,
    )
```

```python
import jax
import jax.numpy as jnp
from jax import lax
from jax.experimental import pallas as pl
from jax.experimental.pallas import tpu as pltpu
from jax.sharding import PartitionSpec as P
import math

RADIUS = 24
CLIP_LIMIT = 0.08
LOW = math.exp(-CLIP_LIMIT)
HIGH = math.exp(CLIP_LIMIT)
MIB = 1 << 20
STEP = 2


def blur_weights(out_index, in_index, extent, radius):
    spread = radius / 3.0
    out_index = out_index[:, None]
    in_index = in_index[None, :]
    distance = (out_index - in_index).astype(jnp.float32)
    inside = (jnp.abs(out_index - in_index) <= radius) & (in_index >= 0) & (in_index < extent)
    kernel = jnp.where(inside, jnp.exp(-distance * distance / (2.0 * spread * spread)), 0.0)
    reach = lax.iota(jnp.int32, 2 * radius + 1)[None, :] - radius
    target = out_index + reach
    valid = (target >= 0) & (target < extent)
    reach_float = reach.astype(jnp.float32)
    weights = jnp.where(valid, jnp.exp(-reach_float * reach_float / (2.0 * spread * spread)), 0.0)
    normaliser = jnp.sum(weights, axis=1, keepdims=True)
    return kernel / normaliser


def halves(value):
    high = value.astype(jnp.bfloat16)
    return high, (value - high.astype(jnp.float32)).astype(jnp.bfloat16)


def split_weights(weights):
    high = lax.reduce_precision(weights, 8, 7)
    return high.astype(jnp.bfloat16), (weights - high).astype(jnp.bfloat16)


def mul(left, right):
    return jnp.dot(left, right, preferred_element_type=jnp.float32)


def row_blur(high_low, low, weight):
    rows = weight.shape[0] // 2
    both = mul(weight[...], high_low)
    return both[:rows] + (both[rows:] + mul(weight[:rows], low))


def column_blur(value, weight_high, weight_low):
    high, low = halves(value)
    return mul(high, weight_high) + (mul(high, weight_low) + mul(low, weight_high))


def advance(blurred, levelled, start, first, last, product, out, put):
    rows = first.shape[0]
    before = last[...]
    running = product[...]
    for plane in range(STEP):
        now = blurred[plane * rows:(plane + 1) * rows]
        ratio = jnp.clip(before / now, LOW, HIGH)
        if plane == 0:
            ratio = jnp.where(start, 1.0, ratio)
            running = jnp.where(start, 1.0, running)

            @pl.when(start)
            def _():
                first[...] = now
        running = running * ratio
        put(out, plane, levelled[plane] * running)
        before = now
    last[...] = before
    product[...] = running


def middle_kernel(volume, flat, row_weight, col_high, col_low, out, first, last, product, inverse):
    start = pl.program_id(0) == 0

    @pl.when(start)
    def _():
        inverse[...] = 1.0 / flat[...]
        last[...] = jnp.ones_like(last)
        product[...] = jnp.ones_like(product)

    count = volume.shape[1]
    levelled, parts = [], []
    for plane in range(STEP):
        value = volume[plane] * inverse[...]
        high, low = halves(value)
        parts.append(row_blur(high, low, row_weight))
        levelled.append(value[RADIUS:count - RADIUS])
    blurred = column_blur(jnp.concatenate(parts, axis=0), col_high[...], col_low[...])

    def put(ref, plane, value):
        ref[plane] = value

    advance(blurred, levelled, start, first, last, product, out, put)


def edge_kernel(top, bottom, above, below, flat_top, flat_bottom, row_weight, col_high, col_low, out, first, last, product, inverse):
    start = pl.program_id(0) == 0
    near = 2 * RADIUS

    @pl.when(start)
    def _():
        inverse[:near] = 1.0 / flat_top[...]
        inverse[near:] = 1.0 / flat_bottom[...]
        last[...] = jnp.ones_like(last)
        product[...] = jnp.ones_like(product)

    levelled, parts = [], []
    for plane in range(STEP):
        upper = top[plane] * inverse[:near]
        lower = bottom[plane] * inverse[near:]
        value = jnp.concatenate([above[plane], upper, lower, below[plane]], axis=0)
        high, low = halves(value)
        parts.append(row_blur(high, low, row_weight))
        levelled.append(jnp.concatenate([upper[:RADIUS], lower[RADIUS:]], axis=0))
    blurred = column_blur(jnp.concatenate(parts, axis=0), col_high[...], col_low[...])

    def put(ref, plane, value):
        ref[plane] = value

    advance(blurred, levelled, start, first, last, product, out, put)


def join_kernel(at_start, before, first_mid, first_edge, product_mid, product_edge, step_out, pieces):
    rows, cols = before.shape
    groups = rows // RADIUS
    lead = at_start[0] == 1
    wide = cols // 4
    for group in range(groups):
        at = pl.ds(group * RADIUS, RADIUS)
        if group == 0:
            edge = pl.ds(0, RADIUS)
        elif group == groups - 1:
            edge = pl.ds(RADIUS, RADIUS)
        else:
            edge = None
        inner = pl.ds((group - 1) * RADIUS, RADIUS)
        first = first_mid[inner] if edge is None else first_edge[edge]
        product = product_mid[inner] if edge is None else product_edge[edge]
        ratio = jnp.where(lead, 1.0, jnp.clip(before[at] / first, LOW, HIGH))
        step_out[at] = ratio
        product = product * ratio
        for part in range(4):
            pieces[group * 4 + part] = product[:, part * wide:(part + 1) * wide]


def scan_kernel(pieces, out):
    running = jnp.ones(pieces.shape[1:], jnp.float32)
    for slab in range(pieces.shape[0]):
        out[slab] = running
        running = running * pieces[slab]


def final_kernel(middle, edge, step, pieces, out, factor):
    rows, cols = step.shape
    wide = cols // 4

    @pl.when(pl.program_id(0) == 0)
    def _():
        for group in range(rows // RADIUS):
            at = pl.ds(group * RADIUS, RADIUS)
            for part in range(4):
                over = pl.ds(part * wide, wide)
                factor[at, over] = step[at, over] * pieces[group * 4 + part]

    for plane in range(out.shape[0]):
        out[plane, :RADIUS] = edge[plane, :RADIUS] * factor[:RADIUS]
        out[plane, RADIUS:rows - RADIUS] = middle[plane] * factor[RADIUS:rows - RADIUS]
        out[plane, rows - RADIUS:] = edge[plane, RADIUS:] * factor[rows - RADIUS:]


def shape(*dims):
    return jax.ShapeDtypeStruct(dims, jnp.float32)


def whole(*dims):
    return pl.BlockSpec(dims, lambda i: (0,) * len(dims))


def params(mib=48):
    return pltpu.CompilerParams(vmem_limit_bytes=mib * MIB)


def middle_call(volume, flat, row_weight, col_high, col_low):
    planes, rows, cols = volume.shape
    inner = rows - 2 * RADIUS
    return pl.pallas_call(
        middle_kernel,
        grid=(planes // STEP,),
        in_specs=[
            pl.BlockSpec((STEP, rows, cols), lambda i: (i, 0, 0)),
            whole(rows, cols),
            whole(*row_weight.shape),
            whole(cols, cols),
            whole(cols, cols),
        ],
        out_specs=[pl.BlockSpec((STEP, inner, cols), lambda i: (i, 0, 0))] + [whole(inner, cols)] * 3,
        out_shape=[shape(planes, inner, cols)] + [shape(inner, cols)] * 3,
        scratch_shapes=[pltpu.VMEM((rows, cols), jnp.float32)],
        compiler_params=params(),
        cost_estimate=pl.CostEstimate(flops=12_000_000_000, bytes_accessed=12_000_000, transcendentals=1_000_000),
    )(volume, flat, row_weight, col_high, col_low)


def edge_call(volume, above, below, flat, row_weight, col_high, col_low):
    planes, rows, cols = volume.shape
    near = 2 * RADIUS
    ends = rows // near - 1
    halo = pl.BlockSpec((STEP, RADIUS, cols), lambda i: (i, 0, 0))
    return pl.pallas_call(
        edge_kernel,
        grid=(planes // STEP,),
        in_specs=[
            pl.BlockSpec((STEP, near, cols), lambda i: (i, 0, 0)),
            pl.BlockSpec((STEP, near, cols), lambda i: (i, ends, 0)),
            halo,
            halo,
            pl.BlockSpec((near, cols), lambda i: (0, 0)),
            pl.BlockSpec((near, cols), lambda i: (ends, 0)),
            whole(*row_weight.shape),
            whole(cols, cols),
            whole(cols, cols),
        ],
        out_specs=[pl.BlockSpec((STEP, near, cols), lambda i: (i, 0, 0))] + [whole(near, cols)] * 3,
        out_shape=[shape(planes, near, cols)] + [shape(near, cols)] * 3,
        scratch_shapes=[pltpu.VMEM((2 * near, cols), jnp.float32)],
        compiler_params=params(),
        cost_estimate=pl.CostEstimate(flops=4_000_000_000, bytes_accessed=8_000_000, transcendentals=400_000),
    )(volume, volume, above, below, flat, flat, row_weight, col_high, col_low)


def final_call(middle, edge, step, pieces):
    planes, inner, cols = middle.shape
    rows = inner + 2 * RADIUS
    group = 4
    return pl.pallas_call(
        final_kernel,
        grid=(planes // group,),
        in_specs=[
            pl.BlockSpec((group, inner, cols), lambda i: (i, 0, 0)),
            pl.BlockSpec((group, 2 * RADIUS, cols), lambda i: (i, 0, 0)),
            whole(rows, cols),
            whole(*pieces.shape),
        ],
        out_specs=pl.BlockSpec((group, rows, cols), lambda i: (i, 0, 0)),
        out_shape=shape(planes, rows, cols),
        scratch_shapes=[pltpu.VMEM((rows, cols), jnp.float32)],
        compiler_params=params(),
    )(middle, edge, step, pieces)


def make_weights(rows, cols, tile_index, extent):
    base = tile_index * rows
    column = blur_weights(lax.iota(jnp.int32, cols), lax.iota(jnp.int32, cols), cols, RADIUS).T
    col_high, col_low = split_weights(column)
    ext = base - RADIUS + lax.iota(jnp.int32, rows + 2 * RADIUS)
    every = blur_weights(base + lax.iota(jnp.int32, rows), ext, extent, RADIUS)
    mid_high, mid_low = split_weights(every[RADIUS:rows - RADIUS, RADIUS:rows + RADIUS])
    near = 3 * RADIUS
    gap = jnp.zeros((RADIUS, near), jnp.float32)
    edge = jnp.concatenate(
        [
            jnp.concatenate([every[:RADIUS, :near], gap], axis=1),
            jnp.concatenate([gap, every[rows - RADIUS:, rows + 2 * RADIUS - near:]], axis=1),
        ],
        axis=0,
    )
    edge_high, edge_low = split_weights(edge)
    return (
        jnp.concatenate([mid_high, mid_low], axis=0),
        jnp.concatenate([edge_high, edge_low], axis=0),
        col_high,
        col_low,
    )


def body(volume, flat_field):
    planes, rows, cols = volume.shape
    tile_index = lax.axis_index("tile")
    depth_index = lax.axis_index("depth")
    tiles, slabs = lax.axis_size("tile"), lax.axis_size("depth")
    top = volume[:, :RADIUS] / flat_field[:RADIUS]
    bottom = volume[:, rows - RADIUS:] / flat_field[rows - RADIUS:]
    above = lax.ppermute(bottom, "tile", [(i, i + 1) for i in range(tiles - 1)])
    below = lax.ppermute(top, "tile", [(i + 1, i) for i in range(tiles - 1)])
    mid_weight, edge_weight, col_high, col_low = make_weights(rows, cols, tile_index, rows * tiles)
    middle, first_mid, last_mid, product_mid = middle_call(volume, flat_field, mid_weight, col_high, col_low)
    edge, first_edge, last_edge, product_edge = edge_call(volume, above, below, flat_field, edge_weight, col_high, col_low)
    deepest = jnp.concatenate([last_edge[:RADIUS], last_mid, last_edge[RADIUS:]], axis=0)
    before = lax.ppermute(deepest, "depth", [(i, i + 1) for i in range(slabs - 1)])
    at_start = (depth_index == 0).astype(jnp.int32).reshape(1)
    vmem = pl.BlockSpec(memory_space=pltpu.VMEM)
    step, pieces = pl.pallas_call(
        join_kernel,
        in_specs=[pl.BlockSpec(memory_space=pltpu.SMEM)] + [vmem] * 5,
        out_specs=[vmem] * 2,
        out_shape=[shape(rows, cols), shape(slabs, RADIUS, cols // 4)],
        compiler_params=params(16),
    )(at_start, before, first_mid, first_edge, product_mid, product_edge)
    mine = lax.all_to_all(pieces, "depth", 0, 0, tiled=True)
    earlier = pl.pallas_call(
        scan_kernel, in_specs=[vmem], out_specs=vmem, out_shape=shape(slabs, RADIUS, cols // 4), compiler_params=params(16)
    )(mine)
    back = lax.all_to_all(earlier, "depth", 0, 0, tiled=True)
    return final_call(middle, edge, step, back)


def solution(mesh):
    return jax.shard_map(
        body,
        mesh=mesh,
        in_specs=(P("depth", "tile", None), P("tile", None)),
        out_specs=P("depth", "tile", None),
        check_vma=False,
    )
```

```python
import jax
import jax.numpy as jnp
from jax import lax
from jax.experimental import pallas as pl
from jax.experimental.pallas import tpu as pltpu
from jax.sharding import PartitionSpec as P
import math

RADIUS = 24
CLIP_LIMIT = 0.08
LOW = math.exp(-CLIP_LIMIT)
HIGH = math.exp(CLIP_LIMIT)
MIB = 1 << 20
STEP = 4
EDGE_STEP = 8
GRANT = 20
TOGETHER = True


def blur_weights(out_index, in_index, extent, radius):
    spread = radius / 3.0
    out_index = out_index[:, None]
    in_index = in_index[None, :]
    distance = (out_index - in_index).astype(jnp.float32)
    inside = (jnp.abs(out_index - in_index) <= radius) & (in_index >= 0) & (in_index < extent)
    kernel = jnp.where(inside, jnp.exp(-distance * distance / (2.0 * spread * spread)), 0.0)
    reach = lax.iota(jnp.int32, 2 * radius + 1)[None, :] - radius
    target = out_index + reach
    valid = (target >= 0) & (target < extent)
    reach_float = reach.astype(jnp.float32)
    weights = jnp.where(valid, jnp.exp(-reach_float * reach_float / (2.0 * spread * spread)), 0.0)
    normaliser = jnp.sum(weights, axis=1, keepdims=True)
    return kernel / normaliser


def halves(value):
    high = value.astype(jnp.bfloat16)
    return high, (value - high.astype(jnp.float32)).astype(jnp.bfloat16)


def split_weights(weights):
    high = lax.reduce_precision(weights, 8, 7)
    return high.astype(jnp.bfloat16), (weights - high).astype(jnp.bfloat16)


def mul(left, right):
    return jnp.dot(left, right, preferred_element_type=jnp.float32)


def row_blur(high, low, weight):
    rows = weight.shape[0] // 2
    both = mul(weight[...], high)
    return both[:rows] + (both[rows:] + mul(weight[:rows], low))


def column_blur(value, weight_high, weight_low):
    high, low = halves(value)
    return mul(high, weight_high) + (mul(high, weight_low) + mul(low, weight_high))


def retreat(blurred, levelled, fresh, later, factor, deepest, out):
    after, running = later[...], factor[...]
    for plane in reversed(range(len(blurred))):
        now = blurred[plane]
        inverse = jnp.clip(after / now, LOW, HIGH)
        if plane == len(blurred) - 1 and fresh is not None:
            inverse = jnp.where(fresh, 1.0, inverse)

            @pl.when(fresh)
            def _():
                deepest[...] = now

        running = running * inverse
        out[plane] = levelled[plane] * running
        after = now
    later[...] = after
    factor[...] = running


def blur_planes(parts, col_high, col_low, together):
    rows = parts[0].shape[0]
    if together:
        blurred = column_blur(jnp.concatenate(parts, axis=0), col_high[...], col_low[...])
        return [blurred[plane * rows:(plane + 1) * rows] for plane in range(len(parts))]
    return [column_blur(part, col_high[...], col_low[...]) for part in parts]


def middle_planes(volume, inverse, row_weight):
    count = volume.shape[1]
    levelled, parts = [], []
    for plane in range(volume.shape[0]):
        value = volume[plane] * inverse[...]
        high, low = halves(value)
        parts.append(row_blur(high, low, row_weight))
        levelled.append(value[RADIUS:count - RADIUS])
    return levelled, parts


def deep_kernel(volume, flat, row_weight, col_high, col_low, out, deepest, later, factor, inverse):
    start = pl.program_id(0) == 0

    @pl.when(start)
    def _():
        inverse[...] = 1.0 / flat[...]
        later[...] = jnp.ones_like(later)
        factor[...] = jnp.ones_like(factor)

    levelled, parts = middle_planes(volume, inverse, row_weight)
    retreat(blur_planes(parts, col_high, col_low, TOGETHER), levelled, start, later, factor, deepest, out)


def shallow_kernel(volume, flat, row_weight, col_high, col_low, later_in, factor_in, out, later, factor, inverse):
    @pl.when(pl.program_id(0) == 0)
    def _():
        inverse[...] = 1.0 / flat[...]
        later[...] = later_in[...]
        factor[...] = factor_in[...]

    levelled, parts = middle_planes(volume, inverse, row_weight)
    retreat(blur_planes(parts, col_high, col_low, TOGETHER), levelled, None, later, factor, None, out)


def edge_kernel(top, bottom, above, below, flat_top, flat_bottom, row_weight, col_high, col_low, out, deepest, later, factor, inverse):
    start = pl.program_id(0) == 0
    near = 2 * RADIUS

    @pl.when(start)
    def _():
        inverse[:near] = 1.0 / flat_top[...]
        inverse[near:] = 1.0 / flat_bottom[...]
        later[...] = jnp.ones_like(later)
        factor[...] = jnp.ones_like(factor)

    levelled, parts = [], []
    for plane in range(top.shape[0]):
        upper = top[plane] * inverse[:near]
        lower = bottom[plane] * inverse[near:]
        value = jnp.concatenate([above[plane], upper, lower, below[plane]], axis=0)
        high, low = halves(value)
        parts.append(row_blur(high, low, row_weight))
        levelled.append(jnp.concatenate([upper[:RADIUS], lower[RADIUS:]], axis=0))
    retreat(blur_planes(parts, col_high, col_low, True), levelled, start, later, factor, deepest, out)


def join_kernel(at_start, before, first_mid, first_edge, factor_mid, factor_edge, pieces):
    rows, cols = before.shape
    groups = rows // RADIUS
    lead = at_start[0] == 1
    wide = cols // 4
    for group in range(groups):
        at = pl.ds(group * RADIUS, RADIUS)
        if group in (0, groups - 1):
            edge = pl.ds(0 if group == 0 else RADIUS, RADIUS)
            first, factor = first_edge[edge], factor_edge[edge]
        else:
            inner = pl.ds((group - 1) * RADIUS, RADIUS)
            first, factor = first_mid[inner], factor_mid[inner]
        total = jnp.where(lead, 1.0, jnp.clip(before[at] / first, LOW, HIGH)) / factor
        for part in range(4):
            pieces[group * 4 + part] = total[:, part * wide:(part + 1) * wide]


def scan_kernel(pieces, out):
    running = jnp.ones(pieces.shape[1:], jnp.float32)
    for slab in range(pieces.shape[0]):
        running = running * pieces[slab]
        out[slab] = running


def final_kernel(shallow, deep, edge, pieces, out, factor):
    step, rows, cols = out.shape
    wide = cols // 4
    at_deep = pl.program_id(0) >= pl.num_programs(0) // 2

    @pl.when(pl.program_id(0) == 0)
    def _():
        for group in range(rows // RADIUS):
            for part in range(4):
                factor[pl.ds(group * RADIUS, RADIUS), pl.ds(part * wide, wide)] = pieces[group * 4 + part]

    inner = pl.ds(RADIUS, rows - 2 * RADIUS)
    for plane in range(step):
        out[plane, :RADIUS] = edge[plane, :RADIUS] * factor[:RADIUS]
        out[plane, rows - RADIUS:] = edge[plane, RADIUS:] * factor[rows - RADIUS:]

    @pl.when(at_deep)
    def _():
        for plane in range(step):
            out[plane, inner] = deep[plane] * factor[inner]

    @pl.when(jnp.logical_not(at_deep))
    def _():
        for plane in range(step):
            out[plane, inner] = shallow[plane] * factor[inner]


def shape(*dims):
    return jax.ShapeDtypeStruct(dims, jnp.float32)


def whole(*dims):
    return pl.BlockSpec(dims, lambda i: (0,) * len(dims))


def params(mib):
    return pltpu.CompilerParams(vmem_limit_bytes=mib * MIB)


def cost(flops, moved):
    return pl.CostEstimate(flops=int(flops), bytes_accessed=int(moved), transcendentals=0)


def deep_call(volume, flat, row_weight, col_high, col_low):
    planes, rows, cols = volume.shape
    inner, half = rows - 2 * RADIUS, planes // 2
    steps = half // STEP
    return pl.pallas_call(
        deep_kernel,
        grid=(steps,),
        in_specs=[
            pl.BlockSpec((STEP, rows, cols), lambda i: (2 * steps - 1 - i, 0, 0)),
            whole(rows, cols),
            whole(*row_weight.shape),
            whole(cols, cols),
            whole(cols, cols),
        ],
        out_specs=[pl.BlockSpec((STEP, inner, cols), lambda i: (steps - 1 - i, 0, 0))] + [whole(inner, cols)] * 3,
        out_shape=[shape(half, inner, cols)] + [shape(inner, cols)] * 3,
        scratch_shapes=[pltpu.VMEM((rows, cols), jnp.float32)],
        compiler_params=params(GRANT),
        cost_estimate=cost(6e9, 6e6),
    )(volume, flat, row_weight, col_high, col_low)


def shallow_call(volume, flat, row_weight, col_high, col_low, later, factor):
    planes, rows, cols = volume.shape
    inner, half = rows - 2 * RADIUS, planes // 2
    steps = half // STEP
    return pl.pallas_call(
        shallow_kernel,
        grid=(steps,),
        in_specs=[
            pl.BlockSpec((STEP, rows, cols), lambda i: (steps - 1 - i, 0, 0)),
            whole(rows, cols),
            whole(*row_weight.shape),
            whole(cols, cols),
            whole(cols, cols),
            whole(inner, cols),
            whole(inner, cols),
        ],
        out_specs=[pl.BlockSpec((STEP, inner, cols), lambda i: (steps - 1 - i, 0, 0))] + [whole(inner, cols)] * 2,
        out_shape=[shape(half, inner, cols)] + [shape(inner, cols)] * 2,
        scratch_shapes=[pltpu.VMEM((rows, cols), jnp.float32)],
        compiler_params=params(GRANT),
        cost_estimate=cost(6e9, 6e6),
    )(volume, flat, row_weight, col_high, col_low, later, factor)


def edge_call(volume, above, below, flat, row_weight, col_high, col_low):
    planes, rows, cols = volume.shape
    near = 2 * RADIUS
    ends = rows // near - 1
    steps = planes // EDGE_STEP
    halo = pl.BlockSpec((EDGE_STEP, RADIUS, cols), lambda i: (steps - 1 - i, 0, 0))
    return pl.pallas_call(
        edge_kernel,
        grid=(steps,),
        in_specs=[
            pl.BlockSpec((EDGE_STEP, near, cols), lambda i: (steps - 1 - i, 0, 0)),
            pl.BlockSpec((EDGE_STEP, near, cols), lambda i: (steps - 1 - i, ends, 0)),
            halo,
            halo,
            pl.BlockSpec((near, cols), lambda i: (0, 0)),
            pl.BlockSpec((near, cols), lambda i: (ends, 0)),
            whole(*row_weight.shape),
            whole(cols, cols),
            whole(cols, cols),
        ],
        out_specs=[pl.BlockSpec((EDGE_STEP, near, cols), lambda i: (steps - 1 - i, 0, 0))] + [whole(near, cols)] * 3,
        out_shape=[shape(planes, near, cols)] + [shape(near, cols)] * 3,
        scratch_shapes=[pltpu.VMEM((2 * near, cols), jnp.float32)],
        compiler_params=params(GRANT),
        cost_estimate=cost(4e9, 8e6),
    )(volume, volume, above, below, flat, flat, row_weight, col_high, col_low)


def final_call(shallow, deep, edge, pieces):
    half, inner, cols = deep.shape
    rows = inner + 2 * RADIUS
    group = 2
    steps = half // group
    return pl.pallas_call(
        final_kernel,
        grid=(2 * steps,),
        in_specs=[
            pl.BlockSpec((group, inner, cols), lambda i: (jnp.minimum(i, steps - 1), 0, 0)),
            pl.BlockSpec((group, inner, cols), lambda i: (jnp.maximum(i - steps, 0), 0, 0)),
            pl.BlockSpec((group, 2 * RADIUS, cols), lambda i: (i, 0, 0)),
            whole(*pieces.shape),
        ],
        out_specs=pl.BlockSpec((group, rows, cols), lambda i: (i, 0, 0)),
        out_shape=shape(2 * half, rows, cols),
        scratch_shapes=[pltpu.VMEM((rows, cols), jnp.float32)],
        compiler_params=params(GRANT),
    )(shallow, deep, edge, pieces)


def make_weights(rows, cols, tile_index, extent):
    base = tile_index * rows
    column = blur_weights(lax.iota(jnp.int32, cols), lax.iota(jnp.int32, cols), cols, RADIUS).T
    col_high, col_low = split_weights(column)
    ext = base - RADIUS + lax.iota(jnp.int32, rows + 2 * RADIUS)
    every = blur_weights(base + lax.iota(jnp.int32, rows), ext, extent, RADIUS)
    mid_high, mid_low = split_weights(every[RADIUS:rows - RADIUS, RADIUS:rows + RADIUS])
    near = 3 * RADIUS
    gap = jnp.zeros((RADIUS, near), jnp.float32)
    edge = jnp.concatenate(
        [
            jnp.concatenate([every[:RADIUS, :near], gap], axis=1),
            jnp.concatenate([gap, every[rows - RADIUS:, rows + 2 * RADIUS - near:]], axis=1),
        ],
        axis=0,
    )
    edge_high, edge_low = split_weights(edge)
    return (
        jnp.concatenate([mid_high, mid_low], axis=0),
        jnp.concatenate([edge_high, edge_low], axis=0),
        col_high,
        col_low,
    )


def body(volume, flat_field):
    planes, rows, cols = volume.shape
    tile_index = lax.axis_index("tile")
    depth_index = lax.axis_index("depth")
    tiles, slabs = lax.axis_size("tile"), lax.axis_size("depth")
    top = volume[:, :RADIUS] / flat_field[:RADIUS]
    bottom = volume[:, rows - RADIUS:] / flat_field[rows - RADIUS:]
    above = lax.ppermute(bottom, "tile", [(i, i + 1) for i in range(tiles - 1)])
    below = lax.ppermute(top, "tile", [(i + 1, i) for i in range(tiles - 1)])
    mid_weight, edge_weight, col_high, col_low = make_weights(rows, cols, tile_index, rows * tiles)
    deep, deepest_mid, later, factor = deep_call(volume, flat_field, mid_weight, col_high, col_low)
    edge, deepest_edge, first_edge, factor_edge = edge_call(volume, above, below, flat_field, edge_weight, col_high, col_low)
    deepest = jnp.concatenate([deepest_edge[:RADIUS], deepest_mid, deepest_edge[RADIUS:]], axis=0)
    before = lax.ppermute(deepest, "depth", [(i, i + 1) for i in range(slabs - 1)])
    shallow, first_mid, factor_mid = shallow_call(volume, flat_field, mid_weight, col_high, col_low, later, factor)
    at_start = (depth_index == 0).astype(jnp.int32).reshape(1)
    vmem = pl.BlockSpec(memory_space=pltpu.VMEM)
    traded = shape(slabs, RADIUS, cols // 4)
    pieces = pl.pallas_call(
        join_kernel,
        in_specs=[pl.BlockSpec(memory_space=pltpu.SMEM)] + [vmem] * 5,
        out_specs=vmem,
        out_shape=traded,
        compiler_params=params(GRANT),
    )(at_start, before, first_mid, first_edge, factor_mid, factor_edge)
    mine = lax.all_to_all(pieces, "depth", 0, 0, tiled=True)
    reached = pl.pallas_call(
        scan_kernel, in_specs=[vmem], out_specs=vmem, out_shape=traded, compiler_params=params(GRANT)
    )(mine)
    back = lax.all_to_all(reached, "depth", 0, 0, tiled=True)
    return final_call(shallow, deep, edge, back)


def solution(mesh):
    return jax.shard_map(
        body,
        mesh=mesh,
        in_specs=(P("depth", "tile", None), P("tile", None)),
        out_specs=P("depth", "tile", None),
        check_vma=False,
    )
```

```python
import jax
import jax.numpy as jnp
from jax import lax
from jax.experimental import pallas as pl
from jax.experimental.pallas import tpu as pltpu
from jax.sharding import PartitionSpec as P
import math

RADIUS = 24
CLIP_LIMIT = 0.08
LOW = math.exp(-CLIP_LIMIT)
HIGH = math.exp(CLIP_LIMIT)
MIB = 1 << 20
STEP = 4
EDGE_STEP = 8
FINAL_STEP = 2
GRANT = 20
LARGE = 60
STREAM = 48
HALO_STEPS = 2
TOGETHER = True


def blur_weights(out_index, in_index, extent, axis):
    spread = RADIUS / 3.0
    distance = (out_index - in_index).astype(jnp.float32)
    inside = (jnp.abs(out_index - in_index) <= RADIUS) & (in_index >= 0) & (in_index < extent)
    kernel = jnp.where(inside, jnp.exp(-distance * distance / (2.0 * spread * spread)), 0.0)
    return kernel / jnp.sum(kernel, axis=axis, keepdims=True)


def numbered(rows, cols):
    return lax.broadcasted_iota(jnp.int32, (rows, cols), 0), lax.broadcasted_iota(jnp.int32, (rows, cols), 1)


def fill_weights(rows, mid_weight, edge_weight, col_high, col_low):
    def put(ref, weights):
        count = weights.shape[0]
        ref[:count], ref[count:] = halves(weights)

    base = lax.axis_index("tile") * rows
    extent = lax.axis_size("tile") * rows
    row, col = numbered(rows - 2 * RADIUS, rows)
    put(mid_weight, blur_weights(base + RADIUS + row, base + col, extent, 1))
    row, col = numbered(2 * RADIUS, 6 * RADIUS)
    row = jnp.where(row < RADIUS, row, row + (rows - 2 * RADIUS))
    col = jnp.where(col < 3 * RADIUS, col, col + (rows - 4 * RADIUS))
    put(edge_weight, blur_weights(base + row, base - RADIUS + col, extent, 1))
    row, col = numbered(*col_high.shape)
    col_high[...], col_low[...] = halves(blur_weights(col, row, col_high.shape[0], 0))


def halves(value):
    high = value.astype(jnp.bfloat16)
    return high, (value - high.astype(jnp.float32)).astype(jnp.bfloat16)


def mul(left, right):
    return jnp.dot(left, right, preferred_element_type=jnp.float32)


def row_blur(high, low, weight):
    rows = weight.shape[0] // 2
    both = mul(weight[...], high)
    return both[:rows] + (both[rows:] + mul(weight[:rows], low))


def column_blur(value, weight_high, weight_low):
    high, low = halves(value)
    return mul(high, weight_high) + (mul(high, weight_low) + mul(low, weight_high))


def retreat(blurred, levelled, fresh, later, factor, deepest, out):
    after, running = later[...], factor[...]
    for plane in reversed(range(len(blurred))):
        now = blurred[plane]
        inverse = jnp.clip(after / now, LOW, HIGH)
        if plane == len(blurred) - 1 and fresh is not None:
            inverse = jnp.where(fresh, 1.0, inverse)

            @pl.when(fresh)
            def _():
                deepest[...] = now

        running = running * inverse
        out[plane] = levelled[plane] * running
        after = now
    later[...] = after
    factor[...] = running


def blur_planes(parts, col_high, col_low, together):
    rows = parts[0].shape[0]
    if together:
        blurred = column_blur(jnp.concatenate(parts, axis=0), col_high[...], col_low[...])
        return [blurred[plane * rows:(plane + 1) * rows] for plane in range(len(parts))]
    return [column_blur(part, col_high[...], col_low[...]) for part in parts]


def middle_planes(volume, inverse, row_weight):
    count = volume.shape[1]
    levelled, parts = [], []
    for plane in range(volume.shape[0]):
        value = volume[plane] * inverse[...]
        high, low = halves(value)
        parts.append(row_blur(high, low, row_weight))
        levelled.append(value[RADIUS:count - RADIUS])
    return levelled, parts


def halo_kernel(upper, lower, flat_top, flat_bottom, top, bottom):
    top[...] = upper[...] / flat_top[...]
    bottom[...] = lower[...] / flat_bottom[...]


def deep_kernel(volume, flat, out, deepest, later, factor, mid_weight, edge_weight, col_high, col_low, inverse):
    start = pl.program_id(0) == 0

    @pl.when(start)
    def _():
        fill_weights(flat.shape[0], mid_weight, edge_weight, col_high, col_low)
        inverse[...] = 1.0 / flat[...]
        later[...] = jnp.ones_like(later)
        factor[...] = jnp.ones_like(factor)

    levelled, parts = middle_planes(volume, inverse, mid_weight)
    retreat(blur_planes(parts, col_high, col_low, TOGETHER), levelled, start, later, factor, deepest, out)


def shallow_kernel(volume, flat, row_weight, col_high, col_low, later_in, factor_in, out, later, factor, inverse):
    @pl.when(pl.program_id(0) == 0)
    def _():
        inverse[...] = 1.0 / flat[...]
        later[...] = later_in[...]
        factor[...] = factor_in[...]

    levelled, parts = middle_planes(volume, inverse, row_weight)
    retreat(blur_planes(parts, col_high, col_low, TOGETHER), levelled, None, later, factor, None, out)


def edge_kernel(top, bottom, above, below, flat_top, flat_bottom, row_weight, col_high, col_low, out, deepest, later, factor, inverse):
    start = pl.program_id(0) == 0
    near = 2 * RADIUS

    @pl.when(start)
    def _():
        inverse[:near] = 1.0 / flat_top[...]
        inverse[near:] = 1.0 / flat_bottom[...]
        later[...] = jnp.ones_like(later)
        factor[...] = jnp.ones_like(factor)

    levelled, parts = [], []
    for plane in range(top.shape[0]):
        upper = top[plane] * inverse[:near]
        lower = bottom[plane] * inverse[near:]
        value = jnp.concatenate([above[plane], upper, lower, below[plane]], axis=0)
        high, low = halves(value)
        parts.append(row_blur(high, low, row_weight))
        levelled.append(jnp.concatenate([upper[:RADIUS], lower[RADIUS:]], axis=0))
    retreat(blur_planes(parts, col_high, col_low, True), levelled, start, later, factor, deepest, out)


def join_kernel(before_mid, before_edge, first_mid, first_edge, factor_mid, factor_edge, pieces):
    inner, cols = before_mid.shape
    groups = inner // RADIUS + 2
    wide = cols // 4
    for group in range(groups):
        if group in (0, groups - 1):
            at = pl.ds(0 if group == 0 else RADIUS, RADIUS)
            before, first, factor = before_edge[at], first_edge[at], factor_edge[at]
        else:
            at = pl.ds((group - 1) * RADIUS, RADIUS)
            before, first, factor = before_mid[at], first_mid[at], factor_mid[at]
        total = jnp.where(before > 0.0, jnp.clip(before / first, LOW, HIGH), 1.0) / factor
        for part in range(4):
            pieces[group * 4 + part] = total[:, part * wide:(part + 1) * wide]


def scan_kernel(pieces, out):
    running = jnp.ones(pieces.shape[1:], jnp.float32)
    for slab in range(pieces.shape[0]):
        running = running * pieces[slab]
        out[slab] = running


def final_kernel(shallow, deep, edge, pieces, out, factor):
    step, rows, cols = out.shape
    wide = cols // 4
    at_deep = pl.program_id(0) >= pl.num_programs(0) // 2

    @pl.when(pl.program_id(0) == 0)
    def _():
        for group in range(rows // RADIUS):
            for part in range(4):
                factor[pl.ds(group * RADIUS, RADIUS), pl.ds(part * wide, wide)] = pieces[group * 4 + part]

    inner = pl.ds(RADIUS, rows - 2 * RADIUS)
    for plane in range(step):
        out[plane, :RADIUS] = edge[plane, :RADIUS] * factor[:RADIUS]
        out[plane, rows - RADIUS:] = edge[plane, RADIUS:] * factor[rows - RADIUS:]

    @pl.when(at_deep)
    def _():
        for plane in range(step):
            out[plane, inner] = deep[plane] * factor[inner]

    @pl.when(jnp.logical_not(at_deep))
    def _():
        for plane in range(step):
            out[plane, inner] = shallow[plane] * factor[inner]


def shape(*dims):
    return jax.ShapeDtypeStruct(dims, jnp.float32)


def whole(*dims):
    return pl.BlockSpec(dims, lambda i: (0,) * len(dims))


def params(mib):
    return pltpu.CompilerParams(vmem_limit_bytes=mib * MIB)


def cost(flops, moved):
    return pl.CostEstimate(flops=int(flops), bytes_accessed=int(moved), transcendentals=0)


def halo_call(volume, flat):
    planes, rows, cols = volume.shape
    ends = rows // RADIUS - 1
    group = planes // HALO_STEPS
    halo = pl.BlockSpec((group, RADIUS, cols), lambda i: (i, 0, 0))
    return pl.pallas_call(
        halo_kernel,
        grid=(HALO_STEPS,),
        in_specs=[
            pl.BlockSpec((group, RADIUS, cols), lambda i: (i, 0, 0)),
            pl.BlockSpec((group, RADIUS, cols), lambda i: (i, ends, 0)),
            pl.BlockSpec((RADIUS, cols), lambda i: (0, 0)),
            pl.BlockSpec((RADIUS, cols), lambda i: (ends, 0)),
        ],
        out_specs=[halo, halo],
        out_shape=[shape(planes, RADIUS, cols)] * 2,
        compiler_params=params(LARGE),
        cost_estimate=cost(1e6, 4e6),
    )(volume, volume, flat, flat)


def deep_call(volume, flat):
    planes, rows, cols = volume.shape
    inner, near, half = rows - 2 * RADIUS, 2 * RADIUS, planes // 2
    steps = half // STEP
    weights = [(2 * inner, rows), (2 * near, 3 * near), (cols, cols), (cols, cols)]
    return pl.pallas_call(
        deep_kernel,
        grid=(steps,),
        in_specs=[pl.BlockSpec((STEP, rows, cols), lambda i: (2 * steps - 1 - i, 0, 0)), whole(rows, cols)],
        out_specs=[pl.BlockSpec((STEP, inner, cols), lambda i: (steps - 1 - i, 0, 0))]
        + [whole(inner, cols)] * 3
        + [whole(*dims) for dims in weights],
        out_shape=[shape(half, inner, cols)]
        + [shape(inner, cols)] * 3
        + [jax.ShapeDtypeStruct(dims, jnp.bfloat16) for dims in weights],
        scratch_shapes=[pltpu.VMEM((rows, cols), jnp.float32)],
        compiler_params=params(STREAM),
        cost_estimate=cost(6e9, 6e6),
    )(volume, flat)


def shallow_call(volume, flat, row_weight, col_high, col_low, later, factor):
    planes, rows, cols = volume.shape
    inner, half = rows - 2 * RADIUS, planes // 2
    steps = half // STEP
    return pl.pallas_call(
        shallow_kernel,
        grid=(steps,),
        in_specs=[
            pl.BlockSpec((STEP, rows, cols), lambda i: (steps - 1 - i, 0, 0)),
            whole(rows, cols),
            whole(*row_weight.shape),
            whole(cols, cols),
            whole(cols, cols),
            whole(inner, cols),
            whole(inner, cols),
        ],
        out_specs=[pl.BlockSpec((STEP, inner, cols), lambda i: (steps - 1 - i, 0, 0))] + [whole(inner, cols)] * 2,
        out_shape=[shape(half, inner, cols)] + [shape(inner, cols)] * 2,
        scratch_shapes=[pltpu.VMEM((rows, cols), jnp.float32)],
        compiler_params=params(STREAM),
        cost_estimate=cost(6e9, 6e6),
    )(volume, flat, row_weight, col_high, col_low, later, factor)


def edge_call(volume, above, below, flat, row_weight, col_high, col_low):
    planes, rows, cols = volume.shape
    near = 2 * RADIUS
    ends = rows // near - 1
    steps = planes // EDGE_STEP
    halo = pl.BlockSpec((EDGE_STEP, RADIUS, cols), lambda i: (steps - 1 - i, 0, 0))
    return pl.pallas_call(
        edge_kernel,
        grid=(steps,),
        in_specs=[
            pl.BlockSpec((EDGE_STEP, near, cols), lambda i: (steps - 1 - i, 0, 0)),
            pl.BlockSpec((EDGE_STEP, near, cols), lambda i: (steps - 1 - i, ends, 0)),
            halo,
            halo,
            pl.BlockSpec((near, cols), lambda i: (0, 0)),
            pl.BlockSpec((near, cols), lambda i: (ends, 0)),
            whole(*row_weight.shape),
            whole(cols, cols),
            whole(cols, cols),
        ],
        out_specs=[pl.BlockSpec((EDGE_STEP, near, cols), lambda i: (steps - 1 - i, 0, 0))] + [whole(near, cols)] * 3,
        out_shape=[shape(planes, near, cols)] + [shape(near, cols)] * 3,
        scratch_shapes=[pltpu.VMEM((2 * near, cols), jnp.float32)],
        compiler_params=params(STREAM),
        cost_estimate=cost(4e9, 8e6),
    )(volume, volume, above, below, flat, flat, row_weight, col_high, col_low)


def final_call(shallow, deep, edge, pieces):
    half, inner, cols = deep.shape
    rows = inner + 2 * RADIUS
    group = 2
    steps = half // group
    return pl.pallas_call(
        final_kernel,
        grid=(2 * steps,),
        in_specs=[
            pl.BlockSpec((group, inner, cols), lambda i: (jnp.minimum(i, steps - 1), 0, 0)),
            pl.BlockSpec((group, inner, cols), lambda i: (jnp.maximum(i - steps, 0), 0, 0)),
            pl.BlockSpec((group, 2 * RADIUS, cols), lambda i: (i, 0, 0)),
            whole(*pieces.shape),
        ],
        out_specs=pl.BlockSpec((group, rows, cols), lambda i: (i, 0, 0)),
        out_shape=shape(2 * half, rows, cols),
        scratch_shapes=[pltpu.VMEM((rows, cols), jnp.float32)],
        compiler_params=params(GRANT),
    )(shallow, deep, edge, pieces)


def body(volume, flat_field):
    planes, rows, cols = volume.shape
    tiles, slabs = lax.axis_size("tile"), lax.axis_size("depth")
    onward = [(i, i + 1) for i in range(slabs - 1)]
    top, bottom = halo_call(volume, flat_field)
    above = lax.ppermute(bottom, "tile", [(i, i + 1) for i in range(tiles - 1)])
    below = lax.ppermute(top, "tile", [(i + 1, i) for i in range(tiles - 1)])
    deep, deepest, later, factor, mid_weight, edge_weight, col_high, col_low = deep_call(volume, flat_field)
    before_mid = lax.ppermute(deepest, "depth", onward)
    edge, deepest_edge, first_edge, factor_edge = edge_call(volume, above, below, flat_field, edge_weight, col_high, col_low)
    before_edge = lax.ppermute(deepest_edge, "depth", onward)
    shallow, first_mid, factor_mid = shallow_call(volume, flat_field, mid_weight, col_high, col_low, later, factor)
    vmem = pl.BlockSpec(memory_space=pltpu.VMEM)
    traded = shape(slabs, RADIUS, cols // 4)
    pieces = pl.pallas_call(
        join_kernel, in_specs=[vmem] * 6, out_specs=vmem, out_shape=traded, compiler_params=params(GRANT)
    )(before_mid, before_edge, first_mid, first_edge, factor_mid, factor_edge)
    mine = lax.all_to_all(pieces, "depth", 0, 0, tiled=True)
    reached = pl.pallas_call(
        scan_kernel, in_specs=[vmem], out_specs=vmem, out_shape=traded, compiler_params=params(GRANT)
    )(mine)
    back = lax.all_to_all(reached, "depth", 0, 0, tiled=True)
    return final_call(shallow, deep, edge, back)


def solution(mesh):
    return jax.shard_map(
        body,
        mesh=mesh,
        in_specs=(P("depth", "tile", None), P("tile", None)),
        out_specs=P("depth", "tile", None),
        check_vma=False,
    )
```

```python
import jax
import jax.numpy as jnp
from jax import lax
from jax.experimental import pallas as pl
from jax.experimental.pallas import tpu as pltpu
from jax.sharding import PartitionSpec as P
import math

RADIUS = 24
CLIP_LIMIT = 0.08
LOW = math.exp(-CLIP_LIMIT)
HIGH = math.exp(CLIP_LIMIT)
MIB = 1 << 20
STEP = 4
EDGE_STEP = 8
FINAL_STEP = 2
GRANT = 20
LARGE = 44


def blur_weights(out_index, in_index, extent, axis):
    spread = RADIUS / 3.0
    distance = (out_index - in_index).astype(jnp.float32)
    inside = (jnp.abs(out_index - in_index) <= RADIUS) & (in_index >= 0) & (in_index < extent)
    kernel = jnp.where(inside, jnp.exp(-distance * distance / (2.0 * spread * spread)), 0.0)
    return kernel / jnp.sum(kernel, axis=axis, keepdims=True)


def numbered(rows, cols):
    return lax.broadcasted_iota(jnp.int32, (rows, cols), 0), lax.broadcasted_iota(jnp.int32, (rows, cols), 1)


def fill_weights(rows, mid_weight, edge_weight, col_high, col_low):
    def put(ref, weights):
        count = weights.shape[0]
        ref[:count], ref[count:] = halves(weights)

    base = lax.axis_index("tile") * rows
    extent = lax.axis_size("tile") * rows
    row, col = numbered(rows - 2 * RADIUS, rows)
    put(mid_weight, blur_weights(base + RADIUS + row, base + col, extent, 1))
    row, col = numbered(2 * RADIUS, 6 * RADIUS)
    row = jnp.where(row < RADIUS, row, row + (rows - 2 * RADIUS))
    col = jnp.where(col < 3 * RADIUS, col, col + (rows - 4 * RADIUS))
    put(edge_weight, blur_weights(base + row, base - RADIUS + col, extent, 1))
    row, col = numbered(*col_high.shape)
    col_high[...], col_low[...] = halves(blur_weights(col, row, col_high.shape[0], 0))


def halves(value):
    high = value.astype(jnp.bfloat16)
    return high, (value - high.astype(jnp.float32)).astype(jnp.bfloat16)


def mul(left, right):
    return jnp.dot(left, right, preferred_element_type=jnp.float32)


def row_blur(high, low, weight):
    rows = weight.shape[0] // 2
    both = mul(weight[...], high)
    return both[:rows] + (both[rows:] + mul(weight[:rows], low))


def column_blur(value, weight_high, weight_low):
    high, low = halves(value)
    return mul(high, weight_high) + (mul(high, weight_low) + mul(low, weight_high))


def retreat(blurred, levelled, fresh, later, factor, put):
    after, running = later[...], factor[...]
    for plane in reversed(range(len(blurred))):
        now = blurred[plane]
        inverse = jnp.clip(after / now, LOW, HIGH)
        if plane == len(blurred) - 1 and fresh is not None:
            inverse = jnp.where(fresh, 1.0, inverse)
        running = running * inverse
        put(plane, levelled[plane] * running)
        after = now
    later[...] = after
    factor[...] = running


def blur_planes(parts, col_high, col_low):
    rows = parts[0].shape[0]
    blurred = column_blur(jnp.concatenate(parts, axis=0), col_high[...], col_low[...])
    return [blurred[plane * rows:(plane + 1) * rows] for plane in range(len(parts))]


def level_kernel(volume, flat, levelled, top, bottom, mid_weight, edge_weight, col_high, col_low, inverse, flat_sem, sems):
    planes, rows, _ = levelled.shape
    first = pltpu.make_async_copy(flat, inverse, flat_sem)
    first.start()
    copies = [pltpu.make_async_copy(volume.at[plane], levelled.at[plane], sems.at[plane]) for plane in range(planes)]
    for copy in copies:
        copy.start()
    fill_weights(rows, mid_weight, edge_weight, col_high, col_low)
    first.wait()
    inverse[...] = 1.0 / inverse[...]
    for plane in range(planes):
        copies[plane].wait()
        value = levelled[plane] * inverse[...]
        levelled[plane] = value
        top[plane] = value[:RADIUS]
        bottom[plane] = value[rows - RADIUS:]


def middle_steps(levelled, row_weight, col_high, col_low, out, later, factor, begin, fresh, deepest):
    rows = levelled.shape[1]
    steps = out.shape[0] // STEP

    def one(index, _):
        at = (steps - 1 - index) * STEP
        values, parts = [], []
        for plane in range(STEP):
            value = levelled[begin + at + plane]
            high, low = halves(value)
            parts.append(row_blur(high, low, row_weight))
            values.append(value[RADIUS:rows - RADIUS])
        blurred = blur_planes(parts, col_high, col_low)
        start = index == 0 if fresh else None
        if fresh:

            @pl.when(start)
            def _():
                deepest[...] = blurred[-1]

        def put(plane, value):
            out[at + plane] = value

        retreat(blurred, values, start, later, factor, put)
        return 0

    lax.fori_loop(0, steps, one, 0)


def deep_kernel(levelled, row_weight, col_high, col_low, out, deepest, later, factor):
    later[...] = jnp.ones_like(later)
    factor[...] = jnp.ones_like(factor)
    begin = levelled.shape[0] - out.shape[0]
    middle_steps(levelled, row_weight, col_high, col_low, out, later, factor, begin, True, deepest)


def shallow_kernel(levelled, row_weight, col_high, col_low, later_in, factor_in, out, later, factor):
    later[...] = later_in[...]
    factor[...] = factor_in[...]
    middle_steps(levelled, row_weight, col_high, col_low, out, later, factor, 0, False, None)


def edge_kernel(levelled, above, below, row_weight, col_high, col_low, out, deepest, later, factor):
    near = 2 * RADIUS
    planes, rows, _ = levelled.shape
    later[...] = jnp.ones_like(later)
    factor[...] = jnp.ones_like(factor)
    steps = planes // EDGE_STEP

    def one(index, _):
        at = (steps - 1 - index) * EDGE_STEP
        values, parts = [], []
        for plane in range(EDGE_STEP):
            upper = levelled[at + plane, :near]
            lower = levelled[at + plane, rows - near:]
            value = jnp.concatenate([above[at + plane], upper, lower, below[at + plane]], axis=0)
            high, low = halves(value)
            parts.append(row_blur(high, low, row_weight))
            values.append(jnp.concatenate([upper[:RADIUS], lower[RADIUS:]], axis=0))
        blurred = blur_planes(parts, col_high, col_low)
        start = index == 0

        @pl.when(start)
        def _():
            deepest[...] = blurred[-1]

        def put(plane, value):
            out[at + plane] = value

        retreat(blurred, values, start, later, factor, put)
        return 0

    lax.fori_loop(0, steps, one, 0)


def join_kernel(before_mid, before_edge, first_mid, first_edge, factor_mid, factor_edge, pieces):
    inner, cols = before_mid.shape
    groups = inner // RADIUS + 2
    wide = cols // 4
    for group in range(groups):
        if group in (0, groups - 1):
            at = pl.ds(0 if group == 0 else RADIUS, RADIUS)
            before, first, factor = before_edge[at], first_edge[at], factor_edge[at]
        else:
            at = pl.ds((group - 1) * RADIUS, RADIUS)
            before, first, factor = before_mid[at], first_mid[at], factor_mid[at]
        total = jnp.where(before > 0.0, jnp.clip(before / first, LOW, HIGH), 1.0) / factor
        for part in range(4):
            pieces[group * 4 + part] = total[:, part * wide:(part + 1) * wide]


def scan_kernel(pieces, out):
    running = jnp.ones(pieces.shape[1:], jnp.float32)
    for slab in range(pieces.shape[0]):
        running = running * pieces[slab]
        out[slab] = running


def final_kernel(shallow, deep, edge, pieces, out, factor):
    step, rows, cols = out.shape
    wide = cols // 4
    index = pl.program_id(0)
    begin = index * step
    half = shallow.shape[0]

    @pl.when(index == 0)
    def _():
        for group in range(rows // RADIUS):
            for part in range(4):
                factor[pl.ds(group * RADIUS, RADIUS), pl.ds(part * wide, wide)] = pieces[group * 4 + part]

    inner = pl.ds(RADIUS, rows - 2 * RADIUS)
    for plane in range(step):
        out[plane, :RADIUS] = edge[begin + plane, :RADIUS] * factor[:RADIUS]
        out[plane, rows - RADIUS:] = edge[begin + plane, RADIUS:] * factor[rows - RADIUS:]

    @pl.when(begin < half)
    def _():
        for plane in range(step):
            out[plane, inner] = shallow[begin + plane] * factor[inner]

    @pl.when(begin >= half)
    def _():
        for plane in range(step):
            out[plane, inner] = deep[begin - half + plane] * factor[inner]


def shape(*dims):
    return jax.ShapeDtypeStruct(dims, jnp.float32)


def params(mib):
    return pltpu.CompilerParams(vmem_limit_bytes=mib * MIB)


def cost(flops, moved):
    return pl.CostEstimate(flops=int(flops), bytes_accessed=int(moved), transcendentals=0)


def vmem_call(kernel, inputs, outputs, given):
    vmem = pl.BlockSpec(memory_space=pltpu.VMEM)
    return pl.pallas_call(
        kernel,
        in_specs=[vmem] * inputs,
        out_specs=[vmem] * len(outputs),
        out_shape=outputs,
        compiler_params=params(GRANT),
        cost_estimate=given,
    )


def level_call(volume, flat):
    planes, rows, cols = volume.shape
    inner, near = rows - 2 * RADIUS, 2 * RADIUS
    weights = [(2 * inner, rows), (2 * near, 3 * near), (cols, cols), (cols, cols)]
    outputs = [shape(planes, rows, cols)] + [shape(planes, RADIUS, cols)] * 2
    outputs += [jax.ShapeDtypeStruct(dims, jnp.bfloat16) for dims in weights]
    return pl.pallas_call(
        level_kernel,
        in_specs=[pl.BlockSpec(memory_space=pltpu.HBM)] * 2,
        out_specs=[pl.BlockSpec(memory_space=pltpu.VMEM)] * len(outputs),
        out_shape=outputs,
        scratch_shapes=[
            pltpu.VMEM((rows, cols), jnp.float32),
            pltpu.SemaphoreType.DMA,
            pltpu.SemaphoreType.DMA((planes,)),
        ],
        compiler_params=params(LARGE),
        cost_estimate=cost(1e7, 7e6),
    )(volume, flat)


def final_call(shallow, deep, edge, pieces):
    half, inner, cols = deep.shape
    rows = inner + 2 * RADIUS
    return pl.pallas_call(
        final_kernel,
        grid=(2 * half // FINAL_STEP,),
        in_specs=[pl.BlockSpec(memory_space=pltpu.VMEM)] * 4,
        out_specs=pl.BlockSpec((FINAL_STEP, rows, cols), lambda i: (i, 0, 0)),
        out_shape=shape(2 * half, rows, cols),
        scratch_shapes=[pltpu.VMEM((rows, cols), jnp.float32)],
        compiler_params=params(GRANT),
    )(shallow, deep, edge, pieces)


def body(volume, flat_field):
    planes, rows, cols = volume.shape
    tiles, slabs = lax.axis_size("tile"), lax.axis_size("depth")
    onward = [(i, i + 1) for i in range(slabs - 1)]
    inner, near, half = rows - 2 * RADIUS, 2 * RADIUS, planes // 2
    levelled, top, bottom, mid_weight, edge_weight, col_high, col_low = level_call(volume, flat_field)
    above = lax.ppermute(bottom, "tile", [(i, i + 1) for i in range(tiles - 1)])
    below = lax.ppermute(top, "tile", [(i + 1, i) for i in range(tiles - 1)])
    deep, deepest, later, factor = vmem_call(
        deep_kernel, 4, [shape(half, inner, cols)] + [shape(inner, cols)] * 3, cost(6e9, 6e6)
    )(levelled, mid_weight, col_high, col_low)
    before_mid = lax.ppermute(deepest, "depth", onward)
    edge, deepest_edge, first_edge, factor_edge = vmem_call(
        edge_kernel, 6, [shape(planes, near, cols)] + [shape(near, cols)] * 3, cost(4e9, 8e6)
    )(levelled, above, below, edge_weight, col_high, col_low)
    before_edge = lax.ppermute(deepest_edge, "depth", onward)
    shallow, first_mid, factor_mid = vmem_call(
        shallow_kernel, 6, [shape(half, inner, cols)] + [shape(inner, cols)] * 2, cost(6e9, 6e6)
    )(levelled, mid_weight, col_high, col_low, later, factor)
    traded = shape(slabs, RADIUS, cols // 4)
    (pieces,) = vmem_call(join_kernel, 6, [traded], cost(1e6, 2e6))(
        before_mid, before_edge, first_mid, first_edge, factor_mid, factor_edge
    )
    mine = lax.all_to_all(pieces, "depth", 0, 0, tiled=True)
    (reached,) = vmem_call(scan_kernel, 1, [traded], cost(1e6, 1e6))(mine)
    back = lax.all_to_all(reached, "depth", 0, 0, tiled=True)
    return final_call(shallow, deep, edge, back)


def solution(mesh):
    return jax.shard_map(
        body,
        mesh=mesh,
        in_specs=(P("depth", "tile", None), P("tile", None)),
        out_specs=P("depth", "tile", None),
        check_vma=False,
    )
```

```python
import jax
import jax.numpy as jnp
from jax import lax
from jax.experimental import pallas as pl
from jax.experimental.pallas import tpu as pltpu
from jax.sharding import PartitionSpec as P
import math

RADIUS = 24
CLIP_LIMIT = 0.08
LOW = math.exp(-CLIP_LIMIT)
HIGH = math.exp(CLIP_LIMIT)
MIB = 1 << 20
STEP = 4
EDGE_STEP = 8
GRANT = 20
LARGE = 44


def blur_weights(out_index, in_index, extent, axis):
    spread = RADIUS / 3.0
    distance = (out_index - in_index).astype(jnp.float32)
    inside = (jnp.abs(out_index - in_index) <= RADIUS) & (in_index >= 0) & (in_index < extent)
    kernel = jnp.where(inside, jnp.exp(-distance * distance / (2.0 * spread * spread)), 0.0)
    return kernel / jnp.sum(kernel, axis=axis, keepdims=True)


def numbered(rows, cols):
    return lax.broadcasted_iota(jnp.int32, (rows, cols), 0), lax.broadcasted_iota(jnp.int32, (rows, cols), 1)


def fill_weights(rows, mid_weight, edge_weight, col_high, col_low):
    def put(ref, weights):
        count = weights.shape[0]
        ref[:count], ref[count:] = halves(weights)

    base = lax.axis_index("tile") * rows
    extent = lax.axis_size("tile") * rows
    row, col = numbered(rows - 2 * RADIUS, rows)
    put(mid_weight, blur_weights(base + RADIUS + row, base + col, extent, 1))
    row, col = numbered(2 * RADIUS, 6 * RADIUS)
    row = jnp.where(row < RADIUS, row, row + (rows - 2 * RADIUS))
    col = jnp.where(col < 3 * RADIUS, col, col + (rows - 4 * RADIUS))
    put(edge_weight, blur_weights(base + row, base - RADIUS + col, extent, 1))
    row, col = numbered(*col_high.shape)
    col_high[...], col_low[...] = halves(blur_weights(col, row, col_high.shape[0], 0))


def halves(value):
    high = value.astype(jnp.bfloat16)
    return high, (value - high.astype(jnp.float32)).astype(jnp.bfloat16)


def mul(left, right):
    return jnp.dot(left, right, preferred_element_type=jnp.float32)


def row_blur(high, low, weight):
    rows = weight.shape[0] // 2
    both = mul(weight[...], high)
    return both[:rows] + (both[rows:] + mul(weight[:rows], low))


def column_blur(value, weight_high, weight_low):
    high, low = halves(value)
    return mul(high, weight_high) + (mul(high, weight_low) + mul(low, weight_high))


def retreat(blurred, levelled, fresh, later, factor, put):
    after, running = later[...], factor[...]
    for plane in reversed(range(len(blurred))):
        now = blurred[plane]
        inverse = jnp.clip(after / now, LOW, HIGH)
        if plane == len(blurred) - 1 and fresh is not None:
            inverse = jnp.where(fresh, 1.0, inverse)
        running = running * inverse
        put(plane, levelled[plane] * running)
        after = now
    later[...] = after
    factor[...] = running


def blur_planes(parts, col_high, col_low):
    rows = parts[0].shape[0]
    blurred = column_blur(jnp.concatenate(parts, axis=0), col_high[...], col_low[...])
    return [blurred[plane * rows:(plane + 1) * rows] for plane in range(len(parts))]


def level_kernel(volume, flat, levelled, top, bottom, mid_weight, edge_weight, col_high, col_low, inverse, flat_sem, sems):
    planes, rows, _ = levelled.shape
    first = pltpu.make_async_copy(flat, inverse, flat_sem)
    first.start()
    copies = [pltpu.make_async_copy(volume.at[plane], levelled.at[plane], sems.at[plane]) for plane in range(planes)]
    for copy in copies:
        copy.start()
    fill_weights(rows, mid_weight, edge_weight, col_high, col_low)
    first.wait()
    inverse[...] = 1.0 / inverse[...]
    for plane in range(planes):
        copies[plane].wait()
        value = levelled[plane] * inverse[...]
        levelled[plane] = value
        top[plane] = value[:RADIUS]
        bottom[plane] = value[rows - RADIUS:]


def middle_steps(levelled, row_weight, col_high, col_low, out, later, factor, begin, fresh, deepest):
    rows = levelled.shape[1]
    steps = out.shape[0] // STEP

    def one(index, _):
        at = (steps - 1 - index) * STEP
        values, parts = [], []
        for plane in range(STEP):
            value = levelled[begin + at + plane]
            high, low = halves(value)
            parts.append(row_blur(high, low, row_weight))
            values.append(value[RADIUS:rows - RADIUS])
        blurred = blur_planes(parts, col_high, col_low)
        start = index == 0 if fresh else None
        if fresh:

            @pl.when(start)
            def _():
                deepest[...] = blurred[-1]

        def put(plane, value):
            out[at + plane] = value

        retreat(blurred, values, start, later, factor, put)
        return 0

    lax.fori_loop(0, steps, one, 0)


def deep_kernel(levelled, row_weight, col_high, col_low, out, deepest, later, factor):
    later[...] = jnp.ones_like(later)
    factor[...] = jnp.ones_like(factor)
    begin = levelled.shape[0] - out.shape[0]
    middle_steps(levelled, row_weight, col_high, col_low, out, later, factor, begin, True, deepest)


def edge_steps(levelled, above, below, row_weight, col_high, col_low, out, later, factor, begin, fresh, deepest):
    near = 2 * RADIUS
    rows = levelled.shape[1]
    steps = out.shape[0] // EDGE_STEP

    def one(index, _):
        at = (steps - 1 - index) * EDGE_STEP
        values, parts = [], []
        for plane in range(EDGE_STEP):
            here = begin + at + plane
            upper = levelled[here, :near]
            lower = levelled[here, rows - near:]
            value = jnp.concatenate([above[here], upper, lower, below[here]], axis=0)
            high, low = halves(value)
            parts.append(row_blur(high, low, row_weight))
            values.append(jnp.concatenate([upper[:RADIUS], lower[RADIUS:]], axis=0))
        blurred = blur_planes(parts, col_high, col_low)
        start = index == 0 if fresh else None
        if fresh:

            @pl.when(start)
            def _():
                deepest[...] = blurred[-1]

        def put(plane, value):
            out[at + plane] = value

        retreat(blurred, values, start, later, factor, put)
        return 0

    lax.fori_loop(0, steps, one, 0)


def edge_kernel(levelled, above, below, row_weight, col_high, col_low, out, deepest, later, factor):
    later[...] = jnp.ones_like(later)
    factor[...] = jnp.ones_like(factor)
    begin = levelled.shape[0] - out.shape[0]
    edge_steps(levelled, above, below, row_weight, col_high, col_low, out, later, factor, begin, True, deepest)


def shallow_kernel(
    levelled, above, below, mid_weight, edge_weight, col_high, col_low, later_mid, factor_mid, later_edge, factor_edge,
    mid_out, mid_later, mid_factor, edge_out, edge_later, edge_factor,
):
    mid_later[...] = later_mid[...]
    mid_factor[...] = factor_mid[...]
    edge_later[...] = later_edge[...]
    edge_factor[...] = factor_edge[...]
    edge_steps(levelled, above, below, edge_weight, col_high, col_low, edge_out, edge_later, edge_factor, 0, False, None)
    middle_steps(levelled, mid_weight, col_high, col_low, mid_out, mid_later, mid_factor, 0, False, None)


def join_kernel(before_mid, before_edge, first_mid, first_edge, factor_mid, factor_edge, pieces):
    inner, cols = before_mid.shape
    groups = inner // RADIUS + 2
    wide = cols // 4
    for group in range(groups):
        if group in (0, groups - 1):
            at = pl.ds(0 if group == 0 else RADIUS, RADIUS)
            before, first, factor = before_edge[at], first_edge[at], factor_edge[at]
        else:
            at = pl.ds((group - 1) * RADIUS, RADIUS)
            before, first, factor = before_mid[at], first_mid[at], factor_mid[at]
        total = jnp.where(before > 0.0, jnp.clip(before / first, LOW, HIGH), 1.0) / factor
        for part in range(4):
            pieces[group * 4 + part] = total[:, part * wide:(part + 1) * wide]


def scan_kernel(pieces, out):
    running = jnp.ones(pieces.shape[1:], jnp.float32)
    for slab in range(pieces.shape[0]):
        running = running * pieces[slab]
        out[slab] = running


def final_kernel(shallow, deep, shallow_edge, deep_edge, pieces, out, factor, result, sems):
    planes, rows, cols = result.shape
    wide = cols // 4
    half = planes // 2
    for group in range(rows // RADIUS):
        for part in range(4):
            factor[group * RADIUS:(group + 1) * RADIUS, part * wide:(part + 1) * wide] = pieces[group * 4 + part]
    copies = []
    for plane in range(planes):
        middle, edge = (shallow, shallow_edge) if plane < half else (deep, deep_edge)
        at = plane % half
        result[plane, :RADIUS] = edge[at, :RADIUS] * factor[:RADIUS]
        result[plane, RADIUS:rows - RADIUS] = middle[at] * factor[RADIUS:rows - RADIUS]
        result[plane, rows - RADIUS:] = edge[at, RADIUS:] * factor[rows - RADIUS:]
        copy = pltpu.make_async_copy(result.at[plane], out.at[plane], sems.at[plane])
        copy.start()
        copies.append(copy)
    for copy in copies:
        copy.wait()


def shape(*dims):
    return jax.ShapeDtypeStruct(dims, jnp.float32)


def params(mib):
    return pltpu.CompilerParams(vmem_limit_bytes=mib * MIB)


def cost(flops, moved):
    return pl.CostEstimate(flops=int(flops), bytes_accessed=int(moved), transcendentals=0)


def vmem_call(kernel, inputs, outputs, given):
    vmem = pl.BlockSpec(memory_space=pltpu.VMEM)
    return pl.pallas_call(
        kernel,
        in_specs=[vmem] * inputs,
        out_specs=[vmem] * len(outputs),
        out_shape=outputs,
        compiler_params=params(GRANT),
        cost_estimate=given,
    )


def level_call(volume, flat):
    planes, rows, cols = volume.shape
    inner, near = rows - 2 * RADIUS, 2 * RADIUS
    weights = [(2 * inner, rows), (2 * near, 3 * near), (cols, cols), (cols, cols)]
    outputs = [shape(planes, rows, cols)] + [shape(planes, RADIUS, cols)] * 2
    outputs += [jax.ShapeDtypeStruct(dims, jnp.bfloat16) for dims in weights]
    return pl.pallas_call(
        level_kernel,
        in_specs=[pl.BlockSpec(memory_space=pltpu.HBM)] * 2,
        out_specs=[pl.BlockSpec(memory_space=pltpu.VMEM)] * len(outputs),
        out_shape=outputs,
        scratch_shapes=[
            pltpu.VMEM((rows, cols), jnp.float32),
            pltpu.SemaphoreType.DMA,
            pltpu.SemaphoreType.DMA((planes,)),
        ],
        compiler_params=params(LARGE),
        cost_estimate=cost(1e7, 7e6),
    )(volume, flat)


def final_call(shallow, deep, shallow_edge, deep_edge, pieces):
    half, inner, cols = deep.shape
    rows = inner + 2 * RADIUS
    return pl.pallas_call(
        final_kernel,
        in_specs=[pl.BlockSpec(memory_space=pltpu.VMEM)] * 5,
        out_specs=pl.BlockSpec(memory_space=pl.ANY),
        out_shape=shape(2 * half, rows, cols),
        scratch_shapes=[
            pltpu.VMEM((rows, cols), jnp.float32),
            pltpu.VMEM((2 * half, rows, cols), jnp.float32),
            pltpu.SemaphoreType.DMA((2 * half,)),
        ],
        compiler_params=params(GRANT),
    )(shallow, deep, shallow_edge, deep_edge, pieces)


def body(volume, flat_field):
    planes, rows, cols = volume.shape
    tiles, slabs = lax.axis_size("tile"), lax.axis_size("depth")
    onward = [(i, i + 1) for i in range(slabs - 1)]
    inner, near, half = rows - 2 * RADIUS, 2 * RADIUS, planes // 2
    levelled, top, bottom, mid_weight, edge_weight, col_high, col_low = level_call(volume, flat_field)
    above = lax.ppermute(bottom, "tile", [(i, i + 1) for i in range(tiles - 1)])
    below = lax.ppermute(top, "tile", [(i + 1, i) for i in range(tiles - 1)])
    deep, deepest, later, factor = vmem_call(
        deep_kernel, 4, [shape(half, inner, cols)] + [shape(inner, cols)] * 3, cost(6e9, 6e6)
    )(levelled, mid_weight, col_high, col_low)
    before_mid = lax.ppermute(deepest, "depth", onward)
    deep_edge, deepest_edge, later_edge, factor_edge = vmem_call(
        edge_kernel, 6, [shape(half, near, cols)] + [shape(near, cols)] * 3, cost(2e9, 4e6)
    )(levelled, above, below, edge_weight, col_high, col_low)
    before_edge = lax.ppermute(deepest_edge, "depth", onward)
    outputs = [shape(half, inner, cols)] + [shape(inner, cols)] * 2 + [shape(half, near, cols)] + [shape(near, cols)] * 2
    shallow, first_mid, factor_mid, shallow_edge, first_edge, factor_edge = vmem_call(shallow_kernel, 11, outputs, cost(8e9, 1e7))(
        levelled, above, below, mid_weight, edge_weight, col_high, col_low, later, factor, later_edge, factor_edge
    )
    traded = shape(slabs, RADIUS, cols // 4)
    (pieces,) = vmem_call(join_kernel, 6, [traded], cost(1e6, 2e6))(
        before_mid, before_edge, first_mid, first_edge, factor_mid, factor_edge
    )
    mine = lax.all_to_all(pieces, "depth", 0, 0, tiled=True)
    (reached,) = vmem_call(scan_kernel, 1, [traded], cost(1e6, 1e6))(mine)
    back = lax.all_to_all(reached, "depth", 0, 0, tiled=True)
    return final_call(shallow, deep, shallow_edge, deep_edge, back)


def solution(mesh):
    return jax.shard_map(
        body,
        mesh=mesh,
        in_specs=(P("depth", "tile", None), P("tile", None)),
        out_specs=P("depth", "tile", None),
        check_vma=False,
    )
```

```python
import jax
import jax.numpy as jnp
from jax import lax
from jax.experimental import pallas as pl
from jax.experimental.pallas import tpu as pltpu
from jax.sharding import PartitionSpec as P
import math

RADIUS = 24
CLIP_LIMIT = 0.08
LOW = math.exp(-CLIP_LIMIT)
HIGH = math.exp(CLIP_LIMIT)
MIB = 1 << 20
STEP = 4
EDGE_STEP = 8
GRANT = 20
LARGE = 44


def blur_weights(out_index, in_index, extent, axis):
    spread = RADIUS / 3.0
    distance = (out_index - in_index).astype(jnp.float32)
    inside = (jnp.abs(out_index - in_index) <= RADIUS) & (in_index >= 0) & (in_index < extent)
    kernel = jnp.where(inside, jnp.exp(-distance * distance / (2.0 * spread * spread)), 0.0)
    return kernel / jnp.sum(kernel, axis=axis, keepdims=True)


def numbered(rows, cols):
    return lax.broadcasted_iota(jnp.int32, (rows, cols), 0), lax.broadcasted_iota(jnp.int32, (rows, cols), 1)


def fill_weights(rows, mid_weight, edge_weight, col_high, col_low):
    def put(ref, weights):
        count = weights.shape[0]
        ref[:count], ref[count:] = halves(weights)

    base = lax.axis_index("tile") * rows
    extent = lax.axis_size("tile") * rows
    row, col = numbered(rows - 2 * RADIUS, rows)
    put(mid_weight, blur_weights(base + RADIUS + row, base + col, extent, 1))
    row, col = numbered(2 * RADIUS, 6 * RADIUS)
    row = jnp.where(row < RADIUS, row, row + (rows - 2 * RADIUS))
    col = jnp.where(col < 3 * RADIUS, col, col + (rows - 4 * RADIUS))
    put(edge_weight, blur_weights(base + row, base - RADIUS + col, extent, 1))
    row, col = numbered(*col_high.shape)
    col_high[...], col_low[...] = halves(blur_weights(col, row, col_high.shape[0], 0))


def halves(value):
    high = value.astype(jnp.bfloat16)
    return high, (value - high.astype(jnp.float32)).astype(jnp.bfloat16)


def mul(left, right):
    return jnp.dot(left, right, preferred_element_type=jnp.float32)


def row_blur(high, low, weight):
    rows = weight.shape[0] // 2
    both = mul(weight[...], high)
    return both[:rows] + (both[rows:] + mul(weight[:rows], low))


def column_blur(value, weight_high, weight_low):
    high, low = halves(value)
    return mul(high, weight_high) + (mul(high, weight_low) + mul(low, weight_high))


def retreat(blurred, levelled, fresh, later, factor, put):
    after, running = later[...], factor[...]
    for plane in reversed(range(len(blurred))):
        now = blurred[plane]
        inverse = jnp.clip(after / now, LOW, HIGH)
        if plane == len(blurred) - 1 and fresh is not None:
            inverse = jnp.where(fresh, 1.0, inverse)
        running = running * inverse
        put(plane, levelled[plane] * running)
        after = now
    later[...] = after
    factor[...] = running


def blur_planes(parts, col_high, col_low):
    rows = parts[0].shape[0]
    blurred = column_blur(jnp.concatenate(parts, axis=0), col_high[...], col_low[...])
    return [blurred[plane * rows:(plane + 1) * rows] for plane in range(len(parts))]


def level_kernel(volume, flat, levelled, outward, inward, mid_weight, edge_weight, col_high, col_low, inverse, flat_sem, sems):
    planes, rows, _ = levelled.shape
    first = pltpu.make_async_copy(flat, inverse, flat_sem)
    first.start()
    copies = [pltpu.make_async_copy(volume.at[plane], levelled.at[plane], sems.at[plane]) for plane in range(planes)]
    for copy in copies:
        copy.start()
    fill_weights(rows, mid_weight, edge_weight, col_high, col_low)
    first.wait()
    inverse[...] = 1.0 / inverse[...]
    odd = lax.axis_index("tile") % 2 == 1
    for plane in range(planes):
        copies[plane].wait()
        value = levelled[plane] * inverse[...]
        levelled[plane] = value
        top, bottom = value[:RADIUS], value[rows - RADIUS:]
        outward[plane] = jnp.where(odd, bottom, top)
        inward[plane] = jnp.where(odd, top, bottom)


def middle_steps(levelled, row_weight, col_high, col_low, out, later, factor, begin, fresh, deepest):
    rows = levelled.shape[1]
    steps = out.shape[0] // STEP

    def one(index, _):
        at = (steps - 1 - index) * STEP
        values, parts = [], []
        for plane in range(STEP):
            value = levelled[begin + at + plane]
            high, low = halves(value)
            parts.append(row_blur(high, low, row_weight))
            values.append(value[RADIUS:rows - RADIUS])
        blurred = blur_planes(parts, col_high, col_low)
        start = index == 0 if fresh else None
        if fresh:

            @pl.when(start)
            def _():
                deepest[...] = blurred[-1]

        def put(plane, value):
            out[at + plane] = value

        retreat(blurred, values, start, later, factor, put)
        return 0

    lax.fori_loop(0, steps, one, 0)


def deep_kernel(levelled, row_weight, col_high, col_low, out, deepest, later, factor):
    later[...] = jnp.ones_like(later)
    factor[...] = jnp.ones_like(factor)
    begin = levelled.shape[0] - out.shape[0]
    middle_steps(levelled, row_weight, col_high, col_low, out, later, factor, begin, True, deepest)


def edge_steps(levelled, outer, inner, row_weight, col_high, col_low, out, later, factor, begin, fresh, deepest):
    near = 2 * RADIUS
    rows = levelled.shape[1]
    steps = out.shape[0] // EDGE_STEP
    odd = lax.axis_index("tile") % 2 == 1

    def one(index, _):
        at = (steps - 1 - index) * EDGE_STEP
        values, parts = [], []
        for plane in range(EDGE_STEP):
            here = begin + at + plane
            upper = levelled[here, :near]
            lower = levelled[here, rows - near:]
            above = jnp.where(odd, inner[here], outer[here])
            below = jnp.where(odd, outer[here], inner[here])
            value = jnp.concatenate([above, upper, lower, below], axis=0)
            high, low = halves(value)
            parts.append(row_blur(high, low, row_weight))
            values.append(jnp.concatenate([upper[:RADIUS], lower[RADIUS:]], axis=0))
        blurred = blur_planes(parts, col_high, col_low)
        start = index == 0 if fresh else None
        if fresh:

            @pl.when(start)
            def _():
                deepest[...] = blurred[-1]

        def put(plane, value):
            out[at + plane] = value

        retreat(blurred, values, start, later, factor, put)
        return 0

    lax.fori_loop(0, steps, one, 0)


def edge_kernel(levelled, outer, inner, row_weight, col_high, col_low, out, deepest, later, factor):
    later[...] = jnp.ones_like(later)
    factor[...] = jnp.ones_like(factor)
    begin = levelled.shape[0] - out.shape[0]
    edge_steps(levelled, outer, inner, row_weight, col_high, col_low, out, later, factor, begin, True, deepest)


def shallow_kernel(
    levelled, outer, inner, mid_weight, edge_weight, col_high, col_low, later_mid, factor_mid, later_edge, factor_edge,
    mid_out, mid_later, mid_factor, edge_out, edge_later, edge_factor,
):
    mid_later[...] = later_mid[...]
    mid_factor[...] = factor_mid[...]
    edge_later[...] = later_edge[...]
    edge_factor[...] = factor_edge[...]
    edge_steps(levelled, outer, inner, edge_weight, col_high, col_low, edge_out, edge_later, edge_factor, 0, False, None)
    middle_steps(levelled, mid_weight, col_high, col_low, mid_out, mid_later, mid_factor, 0, False, None)


def join_kernel(before_mid, before_edge, first_mid, first_edge, factor_mid, factor_edge, pieces):
    inner, cols = before_mid.shape
    groups = inner // RADIUS + 2
    wide = cols // 4
    for group in range(groups):
        if group in (0, groups - 1):
            at = pl.ds(0 if group == 0 else RADIUS, RADIUS)
            before, first, factor = before_edge[at], first_edge[at], factor_edge[at]
        else:
            at = pl.ds((group - 1) * RADIUS, RADIUS)
            before, first, factor = before_mid[at], first_mid[at], factor_mid[at]
        total = jnp.where(before > 0.0, jnp.clip(before / first, LOW, HIGH), 1.0) / factor
        for part in range(4):
            pieces[group * 4 + part] = total[:, part * wide:(part + 1) * wide]


def scan_kernel(pieces, out):
    running = jnp.ones(pieces.shape[1:], jnp.float32)
    for slab in range(pieces.shape[0]):
        running = running * pieces[slab]
        out[slab] = running


def final_kernel(shallow, deep, shallow_edge, deep_edge, pieces, out, factor, result, sems):
    planes, rows, cols = result.shape
    wide = cols // 4
    half = planes // 2
    for group in range(rows // RADIUS):
        for part in range(4):
            factor[group * RADIUS:(group + 1) * RADIUS, part * wide:(part + 1) * wide] = pieces[group * 4 + part]
    copies = []
    for plane in range(planes):
        middle, edge = (shallow, shallow_edge) if plane < half else (deep, deep_edge)
        at = plane % half
        result[plane, :RADIUS] = edge[at, :RADIUS] * factor[:RADIUS]
        result[plane, RADIUS:rows - RADIUS] = middle[at] * factor[RADIUS:rows - RADIUS]
        result[plane, rows - RADIUS:] = edge[at, RADIUS:] * factor[rows - RADIUS:]
        copy = pltpu.make_async_copy(result.at[plane], out.at[plane], sems.at[plane])
        copy.start()
        copies.append(copy)
    for copy in copies:
        copy.wait()


def shape(*dims):
    return jax.ShapeDtypeStruct(dims, jnp.float32)


def params(mib):
    return pltpu.CompilerParams(vmem_limit_bytes=mib * MIB)


def cost(flops, moved):
    return pl.CostEstimate(flops=int(flops), bytes_accessed=int(moved), transcendentals=0)


def vmem_call(kernel, inputs, outputs, given):
    vmem = pl.BlockSpec(memory_space=pltpu.VMEM)
    return pl.pallas_call(
        kernel,
        in_specs=[vmem] * inputs,
        out_specs=[vmem] * len(outputs),
        out_shape=outputs,
        compiler_params=params(GRANT),
        cost_estimate=given,
    )


def level_call(volume, flat):
    planes, rows, cols = volume.shape
    inner, near = rows - 2 * RADIUS, 2 * RADIUS
    weights = [(2 * inner, rows), (2 * near, 3 * near), (cols, cols), (cols, cols)]
    outputs = [shape(planes, rows, cols)] + [shape(planes, RADIUS, cols)] * 2
    outputs += [jax.ShapeDtypeStruct(dims, jnp.bfloat16) for dims in weights]
    return pl.pallas_call(
        level_kernel,
        in_specs=[pl.BlockSpec(memory_space=pltpu.HBM)] * 2,
        out_specs=[pl.BlockSpec(memory_space=pltpu.VMEM)] * len(outputs),
        out_shape=outputs,
        scratch_shapes=[
            pltpu.VMEM((rows, cols), jnp.float32),
            pltpu.SemaphoreType.DMA,
            pltpu.SemaphoreType.DMA((planes,)),
        ],
        compiler_params=params(LARGE),
        cost_estimate=cost(1e7, 7e6),
    )(volume, flat)


def final_call(shallow, deep, shallow_edge, deep_edge, pieces):
    half, inner, cols = deep.shape
    rows = inner + 2 * RADIUS
    return pl.pallas_call(
        final_kernel,
        in_specs=[pl.BlockSpec(memory_space=pltpu.VMEM)] * 5,
        out_specs=pl.BlockSpec(memory_space=pl.ANY),
        out_shape=shape(2 * half, rows, cols),
        scratch_shapes=[
            pltpu.VMEM((rows, cols), jnp.float32),
            pltpu.VMEM((2 * half, rows, cols), jnp.float32),
            pltpu.SemaphoreType.DMA((2 * half,)),
        ],
        compiler_params=params(GRANT),
    )(shallow, deep, shallow_edge, deep_edge, pieces)


def swapped(begin, count):
    return [pair for i in range(begin, count - 1, 2) for pair in ((i, i + 1), (i + 1, i))]


def body(volume, flat_field):
    planes, rows, cols = volume.shape
    tiles, slabs = lax.axis_size("tile"), lax.axis_size("depth")
    onward = [(i, i + 1) for i in range(slabs - 1)]
    inner, near, half = rows - 2 * RADIUS, 2 * RADIUS, planes // 2
    levelled, outward, inward, mid_weight, edge_weight, col_high, col_low = level_call(volume, flat_field)
    outer = lax.ppermute(outward, "tile", swapped(1, tiles))
    inner_halo = lax.ppermute(inward, "tile", swapped(0, tiles))
    deep, deepest, later, factor = vmem_call(
        deep_kernel, 4, [shape(half, inner, cols)] + [shape(inner, cols)] * 3, cost(6e9, 6e6)
    )(levelled, mid_weight, col_high, col_low)
    before_mid = lax.ppermute(deepest, "depth", onward)
    deep_edge, deepest_edge, later_edge, factor_edge = vmem_call(
        edge_kernel, 6, [shape(half, near, cols)] + [shape(near, cols)] * 3, cost(2e9, 4e6)
    )(levelled, outer, inner_halo, edge_weight, col_high, col_low)
    before_edge = lax.ppermute(deepest_edge, "depth", onward)
    outputs = [shape(half, inner, cols)] + [shape(inner, cols)] * 2 + [shape(half, near, cols)] + [shape(near, cols)] * 2
    shallow, first_mid, factor_mid, shallow_edge, first_edge, factor_edge = vmem_call(shallow_kernel, 11, outputs, cost(8e9, 1e7))(
        levelled, outer, inner_halo, mid_weight, edge_weight, col_high, col_low, later, factor, later_edge, factor_edge
    )
    traded = shape(slabs, RADIUS, cols // 4)
    (pieces,) = vmem_call(join_kernel, 6, [traded], cost(1e6, 2e6))(
        before_mid, before_edge, first_mid, first_edge, factor_mid, factor_edge
    )
    mine = lax.all_to_all(pieces, "depth", 0, 0, tiled=True)
    (reached,) = vmem_call(scan_kernel, 1, [traded], cost(1e6, 1e6))(mine)
    back = lax.all_to_all(reached, "depth", 0, 0, tiled=True)
    return final_call(shallow, deep, shallow_edge, deep_edge, back)


def solution(mesh):
    return jax.shard_map(
        body,
        mesh=mesh,
        in_specs=(P("depth", "tile", None), P("tile", None)),
        out_specs=P("depth", "tile", None),
        check_vma=False,
    )
```

```python
import jax
import jax.numpy as jnp
from jax import lax
from jax.experimental import pallas as pl
from jax.experimental.pallas import tpu as pltpu
from jax.sharding import PartitionSpec as P
import math

RADIUS = 24
CLIP_LIMIT = 0.08
LOW = math.exp(-CLIP_LIMIT)
HIGH = math.exp(CLIP_LIMIT)
MIB = 1 << 20
STEP = 4
EDGE_STEP = 8
GRANT = 20
LARGE = 44


def blur_weights(out_index, in_index, extent, axis):
    spread = RADIUS / 3.0
    distance = (out_index - in_index).astype(jnp.float32)
    inside = (jnp.abs(out_index - in_index) <= RADIUS) & (in_index >= 0) & (in_index < extent)
    kernel = jnp.where(inside, jnp.exp(-distance * distance / (2.0 * spread * spread)), 0.0)
    return kernel / jnp.sum(kernel, axis=axis, keepdims=True)


def numbered(rows, cols):
    return lax.broadcasted_iota(jnp.int32, (rows, cols), 0), lax.broadcasted_iota(jnp.int32, (rows, cols), 1)


def fill_weights(rows, mid_weight, edge_weight, col_high, col_low):
    def put(ref, weights):
        count = weights.shape[0]
        ref[:count], ref[count:] = halves(weights)

    base = lax.axis_index("tile") * rows
    extent = lax.axis_size("tile") * rows
    row, col = numbered(rows - 2 * RADIUS, rows)
    put(mid_weight, blur_weights(base + RADIUS + row, base + col, extent, 1))
    row, col = numbered(2 * RADIUS, 6 * RADIUS)
    row = jnp.where(row < RADIUS, row, row + (rows - 2 * RADIUS))
    col = jnp.where(col < 3 * RADIUS, col, col + (rows - 4 * RADIUS))
    put(edge_weight, blur_weights(base + row, base - RADIUS + col, extent, 1))
    row, col = numbered(*col_high.shape)
    col_high[...], col_low[...] = halves(blur_weights(col, row, col_high.shape[0], 0))


def halves(value):
    high = value.astype(jnp.bfloat16)
    return high, (value - high.astype(jnp.float32)).astype(jnp.bfloat16)


def mul(left, right):
    return jnp.dot(left, right, preferred_element_type=jnp.float32)


def row_blur(high, low, weight):
    rows = weight.shape[0] // 2
    both = mul(weight[...], high)
    return both[:rows] + (both[rows:] + mul(weight[:rows], low))


def column_blur(value, weight_high, weight_low):
    high, low = halves(value)
    return mul(high, weight_high) + (mul(high, weight_low) + mul(low, weight_high))


def retreat(blurred, levelled, fresh, later, factor, put):
    after, running = later[...], factor[...]
    for plane in reversed(range(len(blurred))):
        now = blurred[plane]
        inverse = jnp.clip(after / now, LOW, HIGH)
        if plane == len(blurred) - 1 and fresh is not None:
            inverse = jnp.where(fresh, 1.0, inverse)
        running = running * inverse
        put(plane, levelled[plane] * running)
        after = now
    later[...] = after
    factor[...] = running


def blur_planes(parts, col_high, col_low):
    rows = parts[0].shape[0]
    blurred = column_blur(jnp.concatenate(parts, axis=0), col_high[...], col_low[...])
    return [blurred[plane * rows:(plane + 1) * rows] for plane in range(len(parts))]


def level_kernel(volume, flat, levelled, outward, inward, mid_weight, edge_weight, col_high, col_low, inverse, flat_sem, sems):
    planes, rows, _ = levelled.shape
    first = pltpu.make_async_copy(flat, inverse, flat_sem)
    first.start()
    copies = [pltpu.make_async_copy(volume.at[plane], levelled.at[plane], sems.at[plane]) for plane in range(planes)]
    for copy in copies:
        copy.start()
    fill_weights(rows, mid_weight, edge_weight, col_high, col_low)
    first.wait()
    inverse[...] = 1.0 / inverse[...]
    odd = lax.axis_index("tile") % 2 == 1
    for plane in range(planes):
        copies[plane].wait()
        value = levelled[plane] * inverse[...]
        levelled[plane] = value
        top, bottom = value[:RADIUS], value[rows - RADIUS:]
        outward[plane] = jnp.where(odd, bottom, top)
        inward[plane] = jnp.where(odd, top, bottom)


def middle_steps(levelled, row_weight, col_high, col_low, out, later, factor, begin, fresh, deepest):
    rows = levelled.shape[1]
    steps = out.shape[0] // STEP

    def one(index, _):
        at = (steps - 1 - index) * STEP
        values, parts = [], []
        for plane in range(STEP):
            value = levelled[begin + at + plane]
            high, low = halves(value)
            parts.append(row_blur(high, low, row_weight))
            values.append(value[RADIUS:rows - RADIUS])
        blurred = blur_planes(parts, col_high, col_low)
        start = index == 0 if fresh else None
        if fresh:

            @pl.when(start)
            def _():
                deepest[...] = blurred[-1]

        def put(plane, value):
            out[at + plane] = value

        retreat(blurred, values, start, later, factor, put)
        return 0

    lax.fori_loop(0, steps, one, 0)


def deep_kernel(levelled, row_weight, col_high, col_low, out, deepest, later, factor):
    later[...] = jnp.ones_like(later)
    factor[...] = jnp.ones_like(factor)
    begin = levelled.shape[0] - out.shape[0]
    middle_steps(levelled, row_weight, col_high, col_low, out, later, factor, begin, True, deepest)


def edge_steps(levelled, outer, inner, row_weight, col_high, col_low, out, later, factor, begin, fresh, deepest):
    near = 2 * RADIUS
    rows = levelled.shape[1]
    steps = out.shape[0] // EDGE_STEP
    odd = lax.axis_index("tile") % 2 == 1

    def one(index, _):
        at = (steps - 1 - index) * EDGE_STEP
        values, parts = [], []
        for plane in range(EDGE_STEP):
            here = begin + at + plane
            upper = levelled[here, :near]
            lower = levelled[here, rows - near:]
            above = jnp.where(odd, inner[here], outer[here])
            below = jnp.where(odd, outer[here], inner[here])
            value = jnp.concatenate([above, upper, lower, below], axis=0)
            high, low = halves(value)
            parts.append(row_blur(high, low, row_weight))
            values.append(jnp.concatenate([upper[:RADIUS], lower[RADIUS:]], axis=0))
        blurred = blur_planes(parts, col_high, col_low)
        start = index == 0 if fresh else None
        if fresh:

            @pl.when(start)
            def _():
                deepest[...] = blurred[-1]

        def put(plane, value):
            out[at + plane] = value

        retreat(blurred, values, start, later, factor, put)
        return 0

    lax.fori_loop(0, steps, one, 0)


def shallow_planes(
    levelled, outer, inner, mid_weight, edge_weight, col_high, col_low, later_mid, factor_mid, later_edge, factor_edge,
    mid_out, mid_later, mid_factor, edge_out, edge_later, edge_factor,
):
    mid_later[...] = later_mid[...]
    mid_factor[...] = factor_mid[...]
    edge_later[...] = later_edge[...]
    edge_factor[...] = factor_edge[...]
    edge_steps(levelled, outer, inner, edge_weight, col_high, col_low, edge_out, edge_later, edge_factor, 0, False, None)
    middle_steps(levelled, mid_weight, col_high, col_low, mid_out, mid_later, mid_factor, 0, False, None)


def edge_kernel(levelled, outer, inner, mid_weight, edge_weight, col_high, col_low, later_mid, factor_mid, out, deepest, later, factor, *shallow):
    later[...] = jnp.ones_like(later)
    factor[...] = jnp.ones_like(factor)
    begin = levelled.shape[0] - out.shape[0]
    edge_steps(levelled, outer, inner, edge_weight, col_high, col_low, out, later, factor, begin, True, deepest)

    @pl.when(lax.axis_index("tile") % 2 == 1)
    def _():
        shallow_planes(
            levelled, outer, inner, mid_weight, edge_weight, col_high, col_low, later_mid, factor_mid, later, factor, *shallow
        )


def shallow_kernel(*refs):
    given, shallow = refs[:11], refs[17:]

    @pl.when(lax.axis_index("tile") % 2 == 0)
    def _():
        shallow_planes(*given, *shallow)


def join_kernel(before_mid, before_edge, first_mid, first_edge, factor_mid, factor_edge, pieces):
    inner, cols = before_mid.shape
    groups = inner // RADIUS + 2
    wide = cols // 4
    for group in range(groups):
        if group in (0, groups - 1):
            at = pl.ds(0 if group == 0 else RADIUS, RADIUS)
            before, first, factor = before_edge[at], first_edge[at], factor_edge[at]
        else:
            at = pl.ds((group - 1) * RADIUS, RADIUS)
            before, first, factor = before_mid[at], first_mid[at], factor_mid[at]
        total = jnp.where(before > 0.0, jnp.clip(before / first, LOW, HIGH), 1.0) / factor
        for part in range(4):
            pieces[group * 4 + part] = total[:, part * wide:(part + 1) * wide]


def scan_kernel(pieces, out):
    running = jnp.ones(pieces.shape[1:], jnp.float32)
    for slab in range(pieces.shape[0]):
        running = running * pieces[slab]
        out[slab] = running


def final_kernel(shallow, deep, shallow_edge, deep_edge, pieces, out, factor, result, sems):
    planes, rows, cols = result.shape
    wide = cols // 4
    half = planes // 2
    for group in range(rows // RADIUS):
        for part in range(4):
            factor[group * RADIUS:(group + 1) * RADIUS, part * wide:(part + 1) * wide] = pieces[group * 4 + part]
    copies = []
    for plane in range(planes):
        middle, edge = (shallow, shallow_edge) if plane < half else (deep, deep_edge)
        at = plane % half
        result[plane, :RADIUS] = edge[at, :RADIUS] * factor[:RADIUS]
        result[plane, RADIUS:rows - RADIUS] = middle[at] * factor[RADIUS:rows - RADIUS]
        result[plane, rows - RADIUS:] = edge[at, RADIUS:] * factor[rows - RADIUS:]
        copy = pltpu.make_async_copy(result.at[plane], out.at[plane], sems.at[plane])
        copy.start()
        copies.append(copy)
    for copy in copies:
        copy.wait()


def shape(*dims):
    return jax.ShapeDtypeStruct(dims, jnp.float32)


def params(mib):
    return pltpu.CompilerParams(vmem_limit_bytes=mib * MIB)


def cost(flops, moved):
    return pl.CostEstimate(flops=int(flops), bytes_accessed=int(moved), transcendentals=0)


def vmem_call(kernel, inputs, outputs, given, aliases={}):
    vmem = pl.BlockSpec(memory_space=pltpu.VMEM)
    return pl.pallas_call(
        kernel,
        in_specs=[vmem] * inputs,
        out_specs=[vmem] * len(outputs),
        out_shape=outputs,
        input_output_aliases=aliases,
        compiler_params=params(GRANT),
        cost_estimate=given,
    )


def level_call(volume, flat):
    planes, rows, cols = volume.shape
    inner, near = rows - 2 * RADIUS, 2 * RADIUS
    weights = [(2 * inner, rows), (2 * near, 3 * near), (cols, cols), (cols, cols)]
    outputs = [shape(planes, rows, cols)] + [shape(planes, RADIUS, cols)] * 2
    outputs += [jax.ShapeDtypeStruct(dims, jnp.bfloat16) for dims in weights]
    return pl.pallas_call(
        level_kernel,
        in_specs=[pl.BlockSpec(memory_space=pltpu.HBM)] * 2,
        out_specs=[pl.BlockSpec(memory_space=pltpu.VMEM)] * len(outputs),
        out_shape=outputs,
        scratch_shapes=[
            pltpu.VMEM((rows, cols), jnp.float32),
            pltpu.SemaphoreType.DMA,
            pltpu.SemaphoreType.DMA((planes,)),
        ],
        compiler_params=params(LARGE),
        cost_estimate=cost(1e7, 7e6),
    )(volume, flat)


def final_call(shallow, deep, shallow_edge, deep_edge, pieces):
    half, inner, cols = deep.shape
    rows = inner + 2 * RADIUS
    return pl.pallas_call(
        final_kernel,
        in_specs=[pl.BlockSpec(memory_space=pltpu.VMEM)] * 5,
        out_specs=pl.BlockSpec(memory_space=pl.ANY),
        out_shape=shape(2 * half, rows, cols),
        scratch_shapes=[
            pltpu.VMEM((rows, cols), jnp.float32),
            pltpu.VMEM((2 * half, rows, cols), jnp.float32),
            pltpu.SemaphoreType.DMA((2 * half,)),
        ],
        compiler_params=params(GRANT),
    )(shallow, deep, shallow_edge, deep_edge, pieces)


def swapped(begin, count):
    return [pair for i in range(begin, count - 1, 2) for pair in ((i, i + 1), (i + 1, i))]


def body(volume, flat_field):
    planes, rows, cols = volume.shape
    tiles, slabs = lax.axis_size("tile"), lax.axis_size("depth")
    onward = [(i, i + 1) for i in range(slabs - 1)]
    inner, near, half = rows - 2 * RADIUS, 2 * RADIUS, planes // 2
    levelled, outward, inward, mid_weight, edge_weight, col_high, col_low = level_call(volume, flat_field)
    outer = lax.ppermute(outward, "tile", swapped(1, tiles))
    inner_halo = lax.ppermute(inward, "tile", swapped(0, tiles))
    deep, deepest, later, factor = vmem_call(
        deep_kernel, 4, [shape(half, inner, cols)] + [shape(inner, cols)] * 3, cost(6e9, 6e6)
    )(levelled, mid_weight, col_high, col_low)
    before_mid = lax.ppermute(deepest, "depth", onward)
    outputs = [shape(half, inner, cols)] + [shape(inner, cols)] * 2 + [shape(half, near, cols)] + [shape(near, cols)] * 2
    deep_edge, deepest_edge, later_edge, factor_edge, *shallow_parts = vmem_call(
        edge_kernel, 9, [shape(half, near, cols)] + [shape(near, cols)] * 3 + outputs, cost(2e9, 4e6)
    )(levelled, outer, inner_halo, mid_weight, edge_weight, col_high, col_low, later, factor)
    before_edge = lax.ppermute(deepest_edge, "depth", onward)
    shallow, first_mid, factor_mid, shallow_edge, first_edge, factor_edge = vmem_call(
        shallow_kernel, 17, outputs, cost(8e9, 1e7), {11 + i: i for i in range(6)}
    )(
        levelled, outer, inner_halo, mid_weight, edge_weight, col_high, col_low, later, factor, later_edge, factor_edge,
        *shallow_parts,
    )
    traded = shape(slabs, RADIUS, cols // 4)
    (pieces,) = vmem_call(join_kernel, 6, [traded], cost(1e6, 2e6))(
        before_mid, before_edge, first_mid, first_edge, factor_mid, factor_edge
    )
    mine = lax.all_to_all(pieces, "depth", 0, 0, tiled=True)
    (reached,) = vmem_call(scan_kernel, 1, [traded], cost(1e6, 1e6))(mine)
    back = lax.all_to_all(reached, "depth", 0, 0, tiled=True)
    return final_call(shallow, deep, shallow_edge, deep_edge, back)


def solution(mesh):
    return jax.shard_map(
        body,
        mesh=mesh,
        in_specs=(P("depth", "tile", None), P("tile", None)),
        out_specs=P("depth", "tile", None),
        check_vma=False,
    )
```

```python
import jax
import jax.numpy as jnp
from jax import lax
from jax.experimental import pallas as pl
from jax.experimental.pallas import tpu as pltpu
from jax.sharding import PartitionSpec as P
import math

RADIUS = 24
CLIP_LIMIT = 0.08
LOW = math.exp(-CLIP_LIMIT)
HIGH = math.exp(CLIP_LIMIT)
MIB = 1 << 20
STEP = 4
EDGE_STEP = 8
GRANT = 20
LARGE = 36
FIRST = 56


def blur_weights(out_index, in_index, extent, axis):
    spread = RADIUS / 3.0
    distance = (out_index - in_index).astype(jnp.float32)
    inside = (jnp.abs(out_index - in_index) <= RADIUS) & (in_index >= 0) & (in_index < extent)
    kernel = jnp.where(inside, jnp.exp(-distance * distance / (2.0 * spread * spread)), 0.0)
    return kernel / jnp.sum(kernel, axis=axis, keepdims=True)


def numbered(rows, cols):
    return lax.broadcasted_iota(jnp.int32, (rows, cols), 0), lax.broadcasted_iota(jnp.int32, (rows, cols), 1)


def fill_weights(rows, mid_weight, edge_weight, col_high, col_low):
    def put(ref, weights):
        count = weights.shape[0]
        ref[:count], ref[count:] = halves(weights)

    base = lax.axis_index("tile") * rows
    extent = lax.axis_size("tile") * rows
    row, col = numbered(rows - 2 * RADIUS, rows)
    put(mid_weight, blur_weights(base + RADIUS + row, base + col, extent, 1))
    row, col = numbered(2 * RADIUS, 6 * RADIUS)
    row = jnp.where(row < RADIUS, row, row + (rows - 2 * RADIUS))
    col = jnp.where(col < 3 * RADIUS, col, col + (rows - 4 * RADIUS))
    put(edge_weight, blur_weights(base + row, base - RADIUS + col, extent, 1))
    row, col = numbered(*col_high.shape)
    col_high[...], col_low[...] = halves(blur_weights(col, row, col_high.shape[0], 0))


def halves(value):
    high = value.astype(jnp.bfloat16)
    return high, (value - high.astype(jnp.float32)).astype(jnp.bfloat16)


def mul(left, right):
    return jnp.dot(left, right, preferred_element_type=jnp.float32)


def row_blur(high, low, weight):
    rows = weight.shape[0] // 2
    both = mul(weight[...], high)
    return both[:rows] + (both[rows:] + mul(weight[:rows], low))


def column_blur(value, weight_high, weight_low):
    high, low = halves(value)
    return mul(high, weight_high) + (mul(high, weight_low) + mul(low, weight_high))


def retreat(blurred, levelled, fresh, later, factor, put):
    after, running = later[...], factor[...]
    for plane in reversed(range(len(blurred))):
        now = blurred[plane]
        inverse = jnp.clip(after / now, LOW, HIGH)
        if plane == len(blurred) - 1 and fresh is not None:
            inverse = jnp.where(fresh, 1.0, inverse)
        running = running * inverse
        put(plane, levelled[plane] * running)
        after = now
    later[...] = after
    factor[...] = running


def blur_planes(parts, col_high, col_low):
    rows = parts[0].shape[0]
    blurred = column_blur(jnp.concatenate(parts, axis=0), col_high[...], col_low[...])
    return [blurred[plane * rows:(plane + 1) * rows] for plane in range(len(parts))]


def halo_kernel(volume, flat, outward, inward, shade, sems):
    rows = flat.shape[0]
    odd = lax.axis_index("tile") % 2
    near = rows - RADIUS
    copies = []
    for index, (start, ref) in enumerate(((odd * near, outward), (near - odd * near, inward))):
        at = pl.ds(pl.multiple_of(start, RADIUS), RADIUS)
        copies.append(pltpu.make_async_copy(flat.at[at], shade.at[index], sems.at[2 * index]))
        copies.append(pltpu.make_async_copy(volume.at[:, at], ref, sems.at[2 * index + 1]))
    for copy in copies:
        copy.start()
    for copy in copies:
        copy.wait()
    for index, ref in enumerate((outward, inward)):
        inverse = 1.0 / shade[index]
        for plane in range(ref.shape[0]):
            ref[plane] = ref[plane] * inverse


def middle_step(levelled, row_weight, col_high, col_low, begin):
    rows = levelled.shape[1]
    values, parts = [], []
    for plane in range(STEP):
        value = levelled[begin + plane]
        high, low = halves(value)
        parts.append(row_blur(high, low, row_weight))
        values.append(value[RADIUS:rows - RADIUS])
    return values, blur_planes(parts, col_high, col_low)


def deep_kernel(
    volume, flat, levelled, mid_weight, edge_weight, col_high, col_low, out, deepest, later, factor, inverse, flat_sem, sems
):
    planes, rows, _ = levelled.shape
    first = pltpu.make_async_copy(flat, inverse, flat_sem)
    first.start()
    copies = [pltpu.make_async_copy(volume.at[plane], levelled.at[plane], sems.at[plane]) for plane in range(planes)]
    for copy in reversed(copies):
        copy.start()
    fill_weights(rows, mid_weight, edge_weight, col_high, col_low)
    first.wait()
    inverse[...] = 1.0 / inverse[...]
    later[...] = jnp.ones_like(later)
    factor[...] = jnp.ones_like(factor)

    def level(plane):
        copies[plane].wait()
        levelled[plane] = levelled[plane] * inverse[...]

    begin = planes - out.shape[0]
    for at in reversed(range(0, out.shape[0], STEP)):
        for plane in range(STEP):
            level(begin + at + plane)
        values, blurred = middle_step(levelled, mid_weight, col_high, col_low, begin + at)
        fresh = at + STEP == out.shape[0]
        if fresh:
            deepest[...] = blurred[-1]

        def put(plane, value):
            out[at + plane] = value

        retreat(blurred, values, True if fresh else None, later, factor, put)
    for plane in range(begin):
        level(plane)


def middle_steps(levelled, row_weight, col_high, col_low, out, later, factor):
    steps = out.shape[0] // STEP

    def one(index, _):
        at = (steps - 1 - index) * STEP
        values, blurred = middle_step(levelled, row_weight, col_high, col_low, at)

        def put(plane, value):
            out[at + plane] = value

        retreat(blurred, values, None, later, factor, put)
        return 0

    lax.fori_loop(0, steps, one, 0)


def edge_steps(levelled, outer, inner, row_weight, col_high, col_low, out, later, factor, begin, fresh, deepest):
    near = 2 * RADIUS
    rows = levelled.shape[1]
    steps = out.shape[0] // EDGE_STEP
    odd = lax.axis_index("tile") % 2 == 1

    def one(index, _):
        at = (steps - 1 - index) * EDGE_STEP
        values, parts = [], []
        for plane in range(EDGE_STEP):
            here = begin + at + plane
            upper = levelled[here, :near]
            lower = levelled[here, rows - near:]
            above = jnp.where(odd, inner[here], outer[here])
            below = jnp.where(odd, outer[here], inner[here])
            value = jnp.concatenate([above, upper, lower, below], axis=0)
            high, low = halves(value)
            parts.append(row_blur(high, low, row_weight))
            values.append(jnp.concatenate([upper[:RADIUS], lower[RADIUS:]], axis=0))
        blurred = blur_planes(parts, col_high, col_low)
        start = index == 0 if fresh else None
        if fresh:

            @pl.when(start)
            def _():
                deepest[...] = blurred[-1]

        def put(plane, value):
            out[at + plane] = value

        retreat(blurred, values, start, later, factor, put)
        return 0

    lax.fori_loop(0, steps, one, 0)


def edge_kernel(levelled, outer, inner, row_weight, col_high, col_low, out, deepest, later, factor):
    later[...] = jnp.ones_like(later)
    factor[...] = jnp.ones_like(factor)
    begin = levelled.shape[0] - out.shape[0]
    edge_steps(levelled, outer, inner, row_weight, col_high, col_low, out, later, factor, begin, True, deepest)


def shallow_kernel(
    levelled, outer, inner, mid_weight, edge_weight, col_high, col_low, later_mid, factor_mid, later_edge, factor_edge,
    mid_out, mid_later, mid_factor, edge_out, edge_later, edge_factor,
):
    mid_later[...] = later_mid[...]
    mid_factor[...] = factor_mid[...]
    edge_later[...] = later_edge[...]
    edge_factor[...] = factor_edge[...]
    edge_steps(levelled, outer, inner, edge_weight, col_high, col_low, edge_out, edge_later, edge_factor, 0, False, None)
    middle_steps(levelled, mid_weight, col_high, col_low, mid_out, mid_later, mid_factor)


def join_kernel(before_mid, before_edge, first_mid, first_edge, factor_mid, factor_edge, pieces):
    inner, cols = before_mid.shape
    groups = inner // RADIUS + 2
    wide = cols // 4
    for group in range(groups):
        if group in (0, groups - 1):
            at = pl.ds(0 if group == 0 else RADIUS, RADIUS)
            before, first, factor = before_edge[at], first_edge[at], factor_edge[at]
        else:
            at = pl.ds((group - 1) * RADIUS, RADIUS)
            before, first, factor = before_mid[at], first_mid[at], factor_mid[at]
        total = jnp.where(before > 0.0, jnp.clip(before / first, LOW, HIGH), 1.0) / factor
        for part in range(4):
            pieces[group * 4 + part] = total[:, part * wide:(part + 1) * wide]


def scan_kernel(pieces, out):
    running = jnp.ones(pieces.shape[1:], jnp.float32)
    for slab in range(pieces.shape[0]):
        running = running * pieces[slab]
        out[slab] = running


def final_kernel(shallow, deep, shallow_edge, deep_edge, pieces, out, factor, result, sems):
    planes, rows, cols = result.shape
    wide = cols // 4
    half = planes // 2
    for group in range(rows // RADIUS):
        for part in range(4):
            factor[group * RADIUS:(group + 1) * RADIUS, part * wide:(part + 1) * wide] = pieces[group * 4 + part]
    copies = []
    for plane in range(planes):
        middle, edge = (shallow, shallow_edge) if plane < half else (deep, deep_edge)
        at = plane % half
        result[plane, :RADIUS] = edge[at, :RADIUS] * factor[:RADIUS]
        result[plane, RADIUS:rows - RADIUS] = middle[at] * factor[RADIUS:rows - RADIUS]
        result[plane, rows - RADIUS:] = edge[at, RADIUS:] * factor[rows - RADIUS:]
        copy = pltpu.make_async_copy(result.at[plane], out.at[plane], sems.at[plane])
        copy.start()
        copies.append(copy)
    for copy in copies:
        copy.wait()


def shape(*dims):
    return jax.ShapeDtypeStruct(dims, jnp.float32)


def params(mib):
    return pltpu.CompilerParams(vmem_limit_bytes=mib * MIB)


def cost(flops, moved):
    return pl.CostEstimate(flops=int(flops), bytes_accessed=int(moved), transcendentals=0)


def vmem_call(kernel, inputs, outputs, given):
    vmem = pl.BlockSpec(memory_space=pltpu.VMEM)
    return pl.pallas_call(
        kernel,
        in_specs=[vmem] * inputs,
        out_specs=[vmem] * len(outputs),
        out_shape=outputs,
        compiler_params=params(GRANT),
        cost_estimate=given,
    )


def halo_call(volume, flat):
    planes, rows, cols = volume.shape
    return pl.pallas_call(
        halo_kernel,
        in_specs=[pl.BlockSpec(memory_space=pl.ANY)] * 2,
        out_specs=[pl.BlockSpec(memory_space=pltpu.VMEM)] * 2,
        out_shape=[shape(planes, RADIUS, cols)] * 2,
        scratch_shapes=[pltpu.VMEM((2, RADIUS, cols), jnp.float32), pltpu.SemaphoreType.DMA((4,))],
        compiler_params=params(FIRST),
        cost_estimate=cost(1e6, 2e6),
    )(volume, flat)


def deep_call(volume, flat):
    planes, rows, cols = volume.shape
    inner, near, half = rows - 2 * RADIUS, 2 * RADIUS, planes // 2
    weights = [(2 * inner, rows), (2 * near, 3 * near), (cols, cols), (cols, cols)]
    outputs = [shape(planes, rows, cols)]
    outputs += [jax.ShapeDtypeStruct(dims, jnp.bfloat16) for dims in weights]
    outputs += [shape(half, inner, cols)] + [shape(inner, cols)] * 3
    return pl.pallas_call(
        deep_kernel,
        in_specs=[pl.BlockSpec(memory_space=pl.ANY)] * 2,
        out_specs=[pl.BlockSpec(memory_space=pltpu.VMEM)] * len(outputs),
        out_shape=outputs,
        scratch_shapes=[
            pltpu.VMEM((rows, cols), jnp.float32),
            pltpu.SemaphoreType.DMA,
            pltpu.SemaphoreType.DMA((planes,)),
        ],
        compiler_params=params(LARGE),
        cost_estimate=cost(6e9, 7e6),
    )(volume, flat)


def final_call(shallow, deep, shallow_edge, deep_edge, pieces):
    half, inner, cols = deep.shape
    rows = inner + 2 * RADIUS
    return pl.pallas_call(
        final_kernel,
        in_specs=[pl.BlockSpec(memory_space=pltpu.VMEM)] * 5,
        out_specs=pl.BlockSpec(memory_space=pl.ANY),
        out_shape=shape(2 * half, rows, cols),
        scratch_shapes=[
            pltpu.VMEM((rows, cols), jnp.float32),
            pltpu.VMEM((2 * half, rows, cols), jnp.float32),
            pltpu.SemaphoreType.DMA((2 * half,)),
        ],
        compiler_params=params(GRANT),
    )(shallow, deep, shallow_edge, deep_edge, pieces)


def swapped(begin, count):
    return [pair for i in range(begin, count - 1, 2) for pair in ((i, i + 1), (i + 1, i))]


def body(volume, flat_field):
    planes, rows, cols = volume.shape
    tiles, slabs = lax.axis_size("tile"), lax.axis_size("depth")
    onward = [(i, i + 1) for i in range(slabs - 1)]
    inner, near, half = rows - 2 * RADIUS, 2 * RADIUS, planes // 2
    outward, inward = halo_call(volume, flat_field)
    outer = lax.ppermute(outward, "tile", swapped(1, tiles))
    inner_halo = lax.ppermute(inward, "tile", swapped(0, tiles))
    levelled, mid_weight, edge_weight, col_high, col_low, deep, deepest, later, factor = deep_call(volume, flat_field)
    before_mid = lax.ppermute(deepest, "depth", onward)
    deep_edge, deepest_edge, later_edge, factor_edge = vmem_call(
        edge_kernel, 6, [shape(half, near, cols)] + [shape(near, cols)] * 3, cost(2e9, 4e6)
    )(levelled, outer, inner_halo, edge_weight, col_high, col_low)
    before_edge = lax.ppermute(deepest_edge, "depth", onward)
    outputs = [shape(half, inner, cols)] + [shape(inner, cols)] * 2 + [shape(half, near, cols)] + [shape(near, cols)] * 2
    shallow, first_mid, factor_mid, shallow_edge, first_edge, factor_edge = vmem_call(shallow_kernel, 11, outputs, cost(8e9, 1e7))(
        levelled, outer, inner_halo, mid_weight, edge_weight, col_high, col_low, later, factor, later_edge, factor_edge
    )
    traded = shape(slabs, RADIUS, cols // 4)
    (pieces,) = vmem_call(join_kernel, 6, [traded], cost(1e6, 2e6))(
        before_mid, before_edge, first_mid, first_edge, factor_mid, factor_edge
    )
    mine = lax.all_to_all(pieces, "depth", 0, 0, tiled=True)
    (reached,) = vmem_call(scan_kernel, 1, [traded], cost(1e6, 1e6))(mine)
    back = lax.all_to_all(reached, "depth", 0, 0, tiled=True)
    return final_call(shallow, deep, shallow_edge, deep_edge, back)


def solution(mesh):
    return jax.shard_map(
        body,
        mesh=mesh,
        in_specs=(P("depth", "tile", None), P("tile", None)),
        out_specs=P("depth", "tile", None),
        check_vma=False,
    )
```

```python
import jax
import jax.numpy as jnp
from jax import lax
from jax.experimental import pallas as pl
from jax.experimental.pallas import tpu as pltpu
from jax.sharding import PartitionSpec as P
import math

RADIUS = 24
CLIP_LIMIT = 0.08
LOW = math.exp(-CLIP_LIMIT)
HIGH = math.exp(CLIP_LIMIT)
MIB = 1 << 20
STEP = 4
EDGE_STEP = 8
GRANT = 20
FIRST = 56


def blur_weights(out_index, in_index, extent, axis):
    spread = RADIUS / 3.0
    distance = (out_index - in_index).astype(jnp.float32)
    inside = (jnp.abs(out_index - in_index) <= RADIUS) & (in_index >= 0) & (in_index < extent)
    kernel = jnp.where(inside, jnp.exp(-distance * distance / (2.0 * spread * spread)), 0.0)
    return kernel / jnp.sum(kernel, axis=axis, keepdims=True)


def numbered(rows, cols):
    return lax.broadcasted_iota(jnp.int32, (rows, cols), 0), lax.broadcasted_iota(jnp.int32, (rows, cols), 1)


def fill_weights(rows, mid_weight, edge_weight, col_high, col_low):
    def put(ref, weights):
        count = weights.shape[0]
        ref[:count], ref[count:] = halves(weights)

    base = lax.axis_index("tile") * rows
    extent = lax.axis_size("tile") * rows
    row, col = numbered(rows - 2 * RADIUS, rows)
    put(mid_weight, blur_weights(base + RADIUS + row, base + col, extent, 1))
    row, col = numbered(2 * RADIUS, 6 * RADIUS)
    row = jnp.where(row < RADIUS, row, row + (rows - 2 * RADIUS))
    col = jnp.where(col < 3 * RADIUS, col, col + (rows - 4 * RADIUS))
    put(edge_weight, blur_weights(base + row, base - RADIUS + col, extent, 1))
    row, col = numbered(*col_high.shape)
    col_high[...], col_low[...] = halves(blur_weights(col, row, col_high.shape[0], 0))


def halves(value):
    high = value.astype(jnp.bfloat16)
    return high, (value - high.astype(jnp.float32)).astype(jnp.bfloat16)


def mul(left, right):
    return jnp.dot(left, right, preferred_element_type=jnp.float32)


def row_blur(high, low, weight):
    rows = weight.shape[0] // 2
    both = mul(weight[...], high)
    return both[:rows] + (both[rows:] + mul(weight[:rows], low))


def column_blur(value, weight_high, weight_low):
    high, low = halves(value)
    return mul(high, weight_high) + (mul(high, weight_low) + mul(low, weight_high))


def retreat(blurred, levelled, fresh, later, factor, put):
    after, running = later[...], factor[...]
    for plane in reversed(range(len(blurred))):
        now = blurred[plane]
        inverse = jnp.clip(after / now, LOW, HIGH)
        if plane == len(blurred) - 1 and fresh is not None:
            inverse = jnp.where(fresh, 1.0, inverse)
        running = running * inverse
        put(plane, levelled[plane] * running)
        after = now
    later[...] = after
    factor[...] = running


def blur_planes(parts, col_high, col_low):
    rows = parts[0].shape[0]
    blurred = column_blur(jnp.concatenate(parts, axis=0), col_high[...], col_low[...])
    return [blurred[plane * rows:(plane + 1) * rows] for plane in range(len(parts))]


def halo_kernel(volume, flat, outward, inward, shade, sems):
    rows = flat.shape[0]
    odd = lax.axis_index("tile") % 2
    near = rows - RADIUS
    copies = []
    for index, (start, ref) in enumerate(((odd * near, outward), (near - odd * near, inward))):
        at = pl.ds(pl.multiple_of(start, RADIUS), RADIUS)
        copies.append(pltpu.make_async_copy(flat.at[at], shade.at[index], sems.at[2 * index]))
        copies.append(pltpu.make_async_copy(volume.at[:, at], ref, sems.at[2 * index + 1]))
    for copy in copies:
        copy.start()
    for copy in copies:
        copy.wait()
    for index, ref in enumerate((outward, inward)):
        inverse = 1.0 / shade[index]
        for plane in range(ref.shape[0]):
            ref[plane] = ref[plane] * inverse


def middle_step(volume, inverse, row_weight, col_high, col_low, begin):
    rows = volume.shape[1]
    values, parts = [], []
    for plane in range(STEP):
        value = volume[begin + plane] * inverse[...]
        high, low = halves(value)
        parts.append(row_blur(high, low, row_weight))
        values.append(value[RADIUS:rows - RADIUS])
    return values, blur_planes(parts, col_high, col_low)


def deep_kernel(volume, flat, inverse, mid_weight, edge_weight, col_high, col_low, out, deepest, later, factor):
    planes, rows, _ = volume.shape
    fill_weights(rows, mid_weight, edge_weight, col_high, col_low)
    inverse[...] = 1.0 / flat[...]
    later[...] = jnp.ones_like(later)
    factor[...] = jnp.ones_like(factor)
    begin = planes - out.shape[0]
    for at in reversed(range(0, out.shape[0], STEP)):
        values, blurred = middle_step(volume, inverse, mid_weight, col_high, col_low, begin + at)
        fresh = at + STEP == out.shape[0]
        if fresh:
            deepest[...] = blurred[-1]

        def put(plane, value):
            out[at + plane] = value

        retreat(blurred, values, True if fresh else None, later, factor, put)


def middle_steps(volume, inverse, row_weight, col_high, col_low, out, later, factor):
    steps = out.shape[0] // STEP

    def one(index, _):
        at = (steps - 1 - index) * STEP
        values, blurred = middle_step(volume, inverse, row_weight, col_high, col_low, at)

        def put(plane, value):
            out[at + plane] = value

        retreat(blurred, values, None, later, factor, put)
        return 0

    lax.fori_loop(0, steps, one, 0)


def edge_steps(volume, inverse, outer, inner, row_weight, col_high, col_low, out, later, factor, begin, fresh, deepest):
    near = 2 * RADIUS
    rows = volume.shape[1]
    steps = out.shape[0] // EDGE_STEP
    odd = lax.axis_index("tile") % 2 == 1

    def one(index, _):
        at = (steps - 1 - index) * EDGE_STEP
        values, parts = [], []
        for plane in range(EDGE_STEP):
            here = begin + at + plane
            upper = volume[here, :near] * inverse[:near]
            lower = volume[here, rows - near:] * inverse[rows - near:]
            above = jnp.where(odd, inner[here], outer[here])
            below = jnp.where(odd, outer[here], inner[here])
            value = jnp.concatenate([above, upper, lower, below], axis=0)
            high, low = halves(value)
            parts.append(row_blur(high, low, row_weight))
            values.append(jnp.concatenate([upper[:RADIUS], lower[RADIUS:]], axis=0))
        blurred = blur_planes(parts, col_high, col_low)
        start = index == 0 if fresh else None
        if fresh:

            @pl.when(start)
            def _():
                deepest[...] = blurred[-1]

        def put(plane, value):
            out[at + plane] = value

        retreat(blurred, values, start, later, factor, put)
        return 0

    lax.fori_loop(0, steps, one, 0)


def edge_kernel(volume, inverse, outer, inner, row_weight, col_high, col_low, out, deepest, later, factor):
    later[...] = jnp.ones_like(later)
    factor[...] = jnp.ones_like(factor)
    begin = volume.shape[0] - out.shape[0]
    edge_steps(volume, inverse, outer, inner, row_weight, col_high, col_low, out, later, factor, begin, True, deepest)


def shallow_kernel(
    volume, inverse, outer, inner, mid_weight, edge_weight, col_high, col_low, later_mid, factor_mid, later_edge, factor_edge,
    mid_out, mid_later, mid_factor, edge_out, edge_later, edge_factor,
):
    mid_later[...] = later_mid[...]
    mid_factor[...] = factor_mid[...]
    edge_later[...] = later_edge[...]
    edge_factor[...] = factor_edge[...]
    edge_steps(volume, inverse, outer, inner, edge_weight, col_high, col_low, edge_out, edge_later, edge_factor, 0, False, None)
    middle_steps(volume, inverse, mid_weight, col_high, col_low, mid_out, mid_later, mid_factor)


def join_kernel(before_mid, before_edge, first_mid, first_edge, factor_mid, factor_edge, pieces):
    inner, cols = before_mid.shape
    groups = inner // RADIUS + 2
    wide = cols // 4
    for group in range(groups):
        if group in (0, groups - 1):
            at = pl.ds(0 if group == 0 else RADIUS, RADIUS)
            before, first, factor = before_edge[at], first_edge[at], factor_edge[at]
        else:
            at = pl.ds((group - 1) * RADIUS, RADIUS)
            before, first, factor = before_mid[at], first_mid[at], factor_mid[at]
        total = jnp.where(before > 0.0, jnp.clip(before / first, LOW, HIGH), 1.0) / factor
        for part in range(4):
            pieces[group * 4 + part] = total[:, part * wide:(part + 1) * wide]


def scan_kernel(pieces, out):
    running = jnp.ones(pieces.shape[1:], jnp.float32)
    for slab in range(pieces.shape[0]):
        running = running * pieces[slab]
        out[slab] = running


def final_kernel(shallow, deep, shallow_edge, deep_edge, pieces, out, factor, result, sems):
    planes, rows, cols = result.shape
    wide = cols // 4
    half = planes // 2
    for group in range(rows // RADIUS):
        for part in range(4):
            factor[group * RADIUS:(group + 1) * RADIUS, part * wide:(part + 1) * wide] = pieces[group * 4 + part]
    copies = []
    for plane in range(planes):
        middle, edge = (shallow, shallow_edge) if plane < half else (deep, deep_edge)
        at = plane % half
        result[plane, :RADIUS] = edge[at, :RADIUS] * factor[:RADIUS]
        result[plane, RADIUS:rows - RADIUS] = middle[at] * factor[RADIUS:rows - RADIUS]
        result[plane, rows - RADIUS:] = edge[at, RADIUS:] * factor[rows - RADIUS:]
        copy = pltpu.make_async_copy(result.at[plane], out.at[plane], sems.at[plane])
        copy.start()
        copies.append(copy)
    for copy in copies:
        copy.wait()


def shape(*dims):
    return jax.ShapeDtypeStruct(dims, jnp.float32)


def params(mib):
    return pltpu.CompilerParams(vmem_limit_bytes=mib * MIB)


def cost(flops, moved):
    return pl.CostEstimate(flops=int(flops), bytes_accessed=int(moved), transcendentals=0)


def vmem_call(kernel, inputs, outputs, given):
    vmem = pl.BlockSpec(memory_space=pltpu.VMEM)
    return pl.pallas_call(
        kernel,
        in_specs=[vmem] * inputs,
        out_specs=[vmem] * len(outputs),
        out_shape=outputs,
        compiler_params=params(GRANT),
        cost_estimate=given,
    )


def halo_call(volume, flat):
    planes, rows, cols = volume.shape
    return pl.pallas_call(
        halo_kernel,
        in_specs=[pl.BlockSpec(memory_space=pl.ANY)] * 2,
        out_specs=[pl.BlockSpec(memory_space=pltpu.VMEM)] * 2,
        out_shape=[shape(planes, RADIUS, cols)] * 2,
        scratch_shapes=[pltpu.VMEM((2, RADIUS, cols), jnp.float32), pltpu.SemaphoreType.DMA((4,))],
        compiler_params=params(FIRST),
        cost_estimate=cost(1e6, 2e6),
    )(volume, flat)


def deep_call(volume, flat):
    planes, rows, cols = volume.shape
    inner, near, half = rows - 2 * RADIUS, 2 * RADIUS, planes // 2
    weights = [(2 * inner, rows), (2 * near, 3 * near), (cols, cols), (cols, cols)]
    outputs = [shape(rows, cols)]
    outputs += [jax.ShapeDtypeStruct(dims, jnp.bfloat16) for dims in weights]
    outputs += [shape(half, inner, cols)] + [shape(inner, cols)] * 3
    return vmem_call(deep_kernel, 2, outputs, cost(6e9, 7e6))(volume, flat)


def final_call(shallow, deep, shallow_edge, deep_edge, pieces):
    half, inner, cols = deep.shape
    rows = inner + 2 * RADIUS
    return pl.pallas_call(
        final_kernel,
        in_specs=[pl.BlockSpec(memory_space=pltpu.VMEM)] * 5,
        out_specs=pl.BlockSpec(memory_space=pl.ANY),
        out_shape=shape(2 * half, rows, cols),
        scratch_shapes=[
            pltpu.VMEM((rows, cols), jnp.float32),
            pltpu.VMEM((2 * half, rows, cols), jnp.float32),
            pltpu.SemaphoreType.DMA((2 * half,)),
        ],
        compiler_params=params(GRANT),
    )(shallow, deep, shallow_edge, deep_edge, pieces)


def swapped(begin, count):
    return [pair for i in range(begin, count - 1, 2) for pair in ((i, i + 1), (i + 1, i))]


def body(volume, flat_field):
    planes, rows, cols = volume.shape
    tiles, slabs = lax.axis_size("tile"), lax.axis_size("depth")
    onward = [(i, i + 1) for i in range(slabs - 1)]
    inner, near, half = rows - 2 * RADIUS, 2 * RADIUS, planes // 2
    outward, inward = halo_call(volume, flat_field)
    outer = lax.ppermute(outward, "tile", swapped(1, tiles))
    inner_halo = lax.ppermute(inward, "tile", swapped(0, tiles))
    inverse, mid_weight, edge_weight, col_high, col_low, deep, deepest, later, factor = deep_call(volume, flat_field)
    before_mid = lax.ppermute(deepest, "depth", onward)
    deep_edge, deepest_edge, later_edge, factor_edge = vmem_call(
        edge_kernel, 7, [shape(half, near, cols)] + [shape(near, cols)] * 3, cost(2e9, 4e6)
    )(volume, inverse, outer, inner_halo, edge_weight, col_high, col_low)
    before_edge = lax.ppermute(deepest_edge, "depth", onward)
    outputs = [shape(half, inner, cols)] + [shape(inner, cols)] * 2 + [shape(half, near, cols)] + [shape(near, cols)] * 2
    shallow, first_mid, factor_mid, shallow_edge, first_edge, factor_edge = vmem_call(shallow_kernel, 12, outputs, cost(8e9, 1e7))(
        volume, inverse, outer, inner_halo, mid_weight, edge_weight, col_high, col_low, later, factor, later_edge, factor_edge
    )
    traded = shape(slabs, RADIUS, cols // 4)
    (pieces,) = vmem_call(join_kernel, 6, [traded], cost(1e6, 2e6))(
        before_mid, before_edge, first_mid, first_edge, factor_mid, factor_edge
    )
    mine = lax.all_to_all(pieces, "depth", 0, 0, tiled=True)
    (reached,) = vmem_call(scan_kernel, 1, [traded], cost(1e6, 1e6))(mine)
    back = lax.all_to_all(reached, "depth", 0, 0, tiled=True)
    return final_call(shallow, deep, shallow_edge, deep_edge, back)


def solution(mesh):
    return jax.shard_map(
        body,
        mesh=mesh,
        in_specs=(P("depth", "tile", None), P("tile", None)),
        out_specs=P("depth", "tile", None),
        check_vma=False,
    )
```

```python
import functools
import jax
import jax.numpy as jnp
from jax import lax
from jax.experimental import pallas as pl
from jax.experimental.pallas import tpu as pltpu
from jax.sharding import PartitionSpec as P
import math

RADIUS = 24
CLIP_LIMIT = 0.08
LOW = math.exp(-CLIP_LIMIT)
HIGH = math.exp(CLIP_LIMIT)
MIB = 1 << 20
STEP = 4
EDGE_STEP = 8
GRANT = 20
FIRST = 56


def blur_weights(out_index, in_index, extent, axis):
    spread = RADIUS / 3.0
    distance = (out_index - in_index).astype(jnp.float32)
    inside = (jnp.abs(out_index - in_index) <= RADIUS) & (in_index >= 0) & (in_index < extent)
    kernel = jnp.where(inside, jnp.exp(-distance * distance / (2.0 * spread * spread)), 0.0)
    return kernel / jnp.sum(kernel, axis=axis, keepdims=True)


def numbered(rows, cols):
    return lax.broadcasted_iota(jnp.int32, (rows, cols), 0), lax.broadcasted_iota(jnp.int32, (rows, cols), 1)


def fill_weights(rows, mid_weight, edge_weight, col_high, col_low):
    def put(ref, weights):
        count = weights.shape[0]
        ref[:count], ref[count:] = halves(weights)

    base = lax.axis_index("tile") * rows
    extent = lax.axis_size("tile") * rows
    row, col = numbered(rows - 2 * RADIUS, rows)
    put(mid_weight, blur_weights(base + RADIUS + row, base + col, extent, 1))
    row, col = numbered(2 * RADIUS, 6 * RADIUS)
    row = jnp.where(row < RADIUS, row, row + (rows - 2 * RADIUS))
    col = jnp.where(col < 3 * RADIUS, col, col + (rows - 4 * RADIUS))
    put(edge_weight, blur_weights(base + row, base - RADIUS + col, extent, 1))
    row, col = numbered(*col_high.shape)
    col_high[...], col_low[...] = halves(blur_weights(col, row, col_high.shape[0], 0))


def halves(value):
    high = value.astype(jnp.bfloat16)
    return high, (value - high.astype(jnp.float32)).astype(jnp.bfloat16)


def mul(left, right):
    return jnp.dot(left, right, preferred_element_type=jnp.float32)


def row_blur(high, low, weight):
    rows = weight.shape[0] // 2
    both = mul(weight[...], high)
    return both[:rows] + (both[rows:] + mul(weight[:rows], low))


def column_blur(value, weight_high, weight_low):
    high, low = halves(value)
    return mul(high, weight_high) + (mul(high, weight_low) + mul(low, weight_high))


def retreat(blurred, levelled, fresh, later, factor, put):
    after, running = later[...], factor[...]
    for plane in reversed(range(len(blurred))):
        now = blurred[plane]
        inverse = jnp.clip(after / now, LOW, HIGH)
        if plane == len(blurred) - 1 and fresh is not None:
            inverse = jnp.where(fresh, 1.0, inverse)
        running = running * inverse
        put(plane, levelled[plane] * running)
        after = now
    later[...] = after
    factor[...] = running


def blur_planes(parts, col_high, col_low):
    rows = parts[0].shape[0]
    blurred = column_blur(jnp.concatenate(parts, axis=0), col_high[...], col_low[...])
    return [blurred[plane * rows:(plane + 1) * rows] for plane in range(len(parts))]


def halo_kernel(lower, volume, flat, out, shade, sems):
    rows = flat.shape[0]
    start = jnp.where(lax.axis_index("tile") % 2 == lower, rows - RADIUS, 0)
    at = pl.ds(pl.multiple_of(start, RADIUS), RADIUS)
    copies = [pltpu.make_async_copy(flat.at[at], shade, sems.at[0]), pltpu.make_async_copy(volume.at[:, at], out, sems.at[1])]
    for copy in copies:
        copy.start()
    for copy in copies:
        copy.wait()
    inverse = 1.0 / shade[...]
    for plane in range(out.shape[0]):
        out[plane] = out[plane] * inverse


def middle_step(volume, inverse, row_weight, col_high, col_low, begin):
    rows = volume.shape[1]
    values, parts = [], []
    for plane in range(STEP):
        value = volume[begin + plane] * inverse[...]
        high, low = halves(value)
        parts.append(row_blur(high, low, row_weight))
        values.append(value[RADIUS:rows - RADIUS])
    return values, blur_planes(parts, col_high, col_low)


def deep_kernel(volume, flat, inverse, mid_weight, edge_weight, col_high, col_low, out, deepest, later, factor):
    planes, rows, _ = volume.shape
    fill_weights(rows, mid_weight, edge_weight, col_high, col_low)
    inverse[...] = 1.0 / flat[...]
    later[...] = jnp.ones_like(later)
    factor[...] = jnp.ones_like(factor)
    begin = planes - out.shape[0]
    for at in reversed(range(0, out.shape[0], STEP)):
        values, blurred = middle_step(volume, inverse, mid_weight, col_high, col_low, begin + at)
        fresh = at + STEP == out.shape[0]
        if fresh:
            deepest[...] = blurred[-1]

        def put(plane, value):
            out[at + plane] = value

        retreat(blurred, values, True if fresh else None, later, factor, put)


def middle_steps(volume, inverse, row_weight, col_high, col_low, out, later, factor):
    steps = out.shape[0] // STEP

    def one(index, _):
        at = (steps - 1 - index) * STEP
        values, blurred = middle_step(volume, inverse, row_weight, col_high, col_low, at)

        def put(plane, value):
            out[at + plane] = value

        retreat(blurred, values, None, later, factor, put)
        return 0

    lax.fori_loop(0, steps, one, 0)


def edge_steps(volume, inverse, outer, inner, row_weight, col_high, col_low, out, later, factor, begin, fresh, deepest):
    near = 2 * RADIUS
    rows = volume.shape[1]
    steps = out.shape[0] // EDGE_STEP
    odd = lax.axis_index("tile") % 2 == 1

    def one(index, _):
        at = (steps - 1 - index) * EDGE_STEP
        values, parts = [], []
        for plane in range(EDGE_STEP):
            here = begin + at + plane
            upper = volume[here, :near] * inverse[:near]
            lower = volume[here, rows - near:] * inverse[rows - near:]
            above = jnp.where(odd, inner[here], outer[here])
            below = jnp.where(odd, outer[here], inner[here])
            value = jnp.concatenate([above, upper, lower, below], axis=0)
            high, low = halves(value)
            parts.append(row_blur(high, low, row_weight))
            values.append(jnp.concatenate([upper[:RADIUS], lower[RADIUS:]], axis=0))
        blurred = blur_planes(parts, col_high, col_low)
        start = index == 0 if fresh else None
        if fresh:

            @pl.when(start)
            def _():
                deepest[...] = blurred[-1]

        def put(plane, value):
            out[at + plane] = value

        retreat(blurred, values, start, later, factor, put)
        return 0

    lax.fori_loop(0, steps, one, 0)


def edge_kernel(volume, inverse, outer, inner, row_weight, col_high, col_low, out, deepest, later, factor):
    later[...] = jnp.ones_like(later)
    factor[...] = jnp.ones_like(factor)
    begin = volume.shape[0] - out.shape[0]
    edge_steps(volume, inverse, outer, inner, row_weight, col_high, col_low, out, later, factor, begin, True, deepest)


def shallow_kernel(
    volume, inverse, outer, inner, mid_weight, edge_weight, col_high, col_low, later_mid, factor_mid, later_edge, factor_edge,
    mid_out, mid_later, mid_factor, edge_out, edge_later, edge_factor,
):
    mid_later[...] = later_mid[...]
    mid_factor[...] = factor_mid[...]
    edge_later[...] = later_edge[...]
    edge_factor[...] = factor_edge[...]
    edge_steps(volume, inverse, outer, inner, edge_weight, col_high, col_low, edge_out, edge_later, edge_factor, 0, False, None)
    middle_steps(volume, inverse, mid_weight, col_high, col_low, mid_out, mid_later, mid_factor)


def join_kernel(before_mid, before_edge, first_mid, first_edge, factor_mid, factor_edge, pieces):
    inner, cols = before_mid.shape
    groups = inner // RADIUS + 2
    wide = cols // 4
    for group in range(groups):
        if group in (0, groups - 1):
            at = pl.ds(0 if group == 0 else RADIUS, RADIUS)
            before, first, factor = before_edge[at], first_edge[at], factor_edge[at]
        else:
            at = pl.ds((group - 1) * RADIUS, RADIUS)
            before, first, factor = before_mid[at], first_mid[at], factor_mid[at]
        total = jnp.where(before > 0.0, jnp.clip(before / first, LOW, HIGH), 1.0) / factor
        for part in range(4):
            pieces[group * 4 + part] = total[:, part * wide:(part + 1) * wide]


def scan_kernel(pieces, out):
    running = jnp.ones(pieces.shape[1:], jnp.float32)
    for slab in range(pieces.shape[0]):
        running = running * pieces[slab]
        out[slab] = running


def final_kernel(shallow, deep, shallow_edge, deep_edge, pieces, out, factor, result, sems):
    planes, rows, cols = result.shape
    wide = cols // 4
    half = planes // 2
    for group in range(rows // RADIUS):
        for part in range(4):
            factor[group * RADIUS:(group + 1) * RADIUS, part * wide:(part + 1) * wide] = pieces[group * 4 + part]
    copies = []
    for plane in range(planes):
        middle, edge = (shallow, shallow_edge) if plane < half else (deep, deep_edge)
        at = plane % half
        result[plane, :RADIUS] = edge[at, :RADIUS] * factor[:RADIUS]
        result[plane, RADIUS:rows - RADIUS] = middle[at] * factor[RADIUS:rows - RADIUS]
        result[plane, rows - RADIUS:] = edge[at, RADIUS:] * factor[rows - RADIUS:]
        copy = pltpu.make_async_copy(result.at[plane], out.at[plane], sems.at[plane])
        copy.start()
        copies.append(copy)
    for copy in copies:
        copy.wait()


def shape(*dims):
    return jax.ShapeDtypeStruct(dims, jnp.float32)


def params(mib):
    return pltpu.CompilerParams(vmem_limit_bytes=mib * MIB)


def cost(flops, moved):
    return pl.CostEstimate(flops=int(flops), bytes_accessed=int(moved), transcendentals=0)


def vmem_call(kernel, inputs, outputs, given):
    vmem = pl.BlockSpec(memory_space=pltpu.VMEM)
    return pl.pallas_call(
        kernel,
        in_specs=[vmem] * inputs,
        out_specs=[vmem] * len(outputs),
        out_shape=outputs,
        compiler_params=params(GRANT),
        cost_estimate=given,
    )


def halo_call(volume, flat, lower):
    planes, rows, cols = volume.shape
    return pl.pallas_call(
        functools.partial(halo_kernel, lower),
        in_specs=[pl.BlockSpec(memory_space=pl.ANY)] * 2,
        out_specs=pl.BlockSpec(memory_space=pltpu.VMEM),
        out_shape=shape(planes, RADIUS, cols),
        scratch_shapes=[pltpu.VMEM((RADIUS, cols), jnp.float32), pltpu.SemaphoreType.DMA((2,))],
        compiler_params=params(FIRST),
        cost_estimate=cost(1e6, 2e6),
    )(volume, flat)


def deep_call(volume, flat):
    planes, rows, cols = volume.shape
    inner, near, half = rows - 2 * RADIUS, 2 * RADIUS, planes // 2
    weights = [(2 * inner, rows), (2 * near, 3 * near), (cols, cols), (cols, cols)]
    outputs = [shape(rows, cols)]
    outputs += [jax.ShapeDtypeStruct(dims, jnp.bfloat16) for dims in weights]
    outputs += [shape(half, inner, cols)] + [shape(inner, cols)] * 3
    return vmem_call(deep_kernel, 2, outputs, cost(6e9, 7e6))(volume, flat)


def final_call(shallow, deep, shallow_edge, deep_edge, pieces):
    half, inner, cols = deep.shape
    rows = inner + 2 * RADIUS
    return pl.pallas_call(
        final_kernel,
        in_specs=[pl.BlockSpec(memory_space=pltpu.VMEM)] * 5,
        out_specs=pl.BlockSpec(memory_space=pl.ANY),
        out_shape=shape(2 * half, rows, cols),
        scratch_shapes=[
            pltpu.VMEM((rows, cols), jnp.float32),
            pltpu.VMEM((2 * half, rows, cols), jnp.float32),
            pltpu.SemaphoreType.DMA((2 * half,)),
        ],
        compiler_params=params(GRANT),
    )(shallow, deep, shallow_edge, deep_edge, pieces)


def swapped(begin, count):
    return [pair for i in range(begin, count - 1, 2) for pair in ((i, i + 1), (i + 1, i))]


def body(volume, flat_field):
    planes, rows, cols = volume.shape
    tiles, slabs = lax.axis_size("tile"), lax.axis_size("depth")
    onward = [(i, i + 1) for i in range(slabs - 1)]
    inner, near, half = rows - 2 * RADIUS, 2 * RADIUS, planes // 2
    outer = lax.ppermute(halo_call(volume, flat_field, 1), "tile", swapped(1, tiles))
    inner_halo = lax.ppermute(halo_call(volume, flat_field, 0), "tile", swapped(0, tiles))
    inverse, mid_weight, edge_weight, col_high, col_low, deep, deepest, later, factor = deep_call(volume, flat_field)
    before_mid = lax.ppermute(deepest, "depth", onward)
    deep_edge, deepest_edge, later_edge, factor_edge = vmem_call(
        edge_kernel, 7, [shape(half, near, cols)] + [shape(near, cols)] * 3, cost(2e9, 4e6)
    )(volume, inverse, outer, inner_halo, edge_weight, col_high, col_low)
    before_edge = lax.ppermute(deepest_edge, "depth", onward)
    outputs = [shape(half, inner, cols)] + [shape(inner, cols)] * 2 + [shape(half, near, cols)] + [shape(near, cols)] * 2
    shallow, first_mid, factor_mid, shallow_edge, first_edge, factor_edge = vmem_call(shallow_kernel, 12, outputs, cost(8e9, 1e7))(
        volume, inverse, outer, inner_halo, mid_weight, edge_weight, col_high, col_low, later, factor, later_edge, factor_edge
    )
    traded = shape(slabs, RADIUS, cols // 4)
    (pieces,) = vmem_call(join_kernel, 6, [traded], cost(1e6, 2e6))(
        before_mid, before_edge, first_mid, first_edge, factor_mid, factor_edge
    )
    mine = lax.all_to_all(pieces, "depth", 0, 0, tiled=True)
    (reached,) = vmem_call(scan_kernel, 1, [traded], cost(1e6, 1e6))(mine)
    back = lax.all_to_all(reached, "depth", 0, 0, tiled=True)
    return final_call(shallow, deep, shallow_edge, deep_edge, back)


def solution(mesh):
    return jax.shard_map(
        body,
        mesh=mesh,
        in_specs=(P("depth", "tile", None), P("tile", None)),
        out_specs=P("depth", "tile", None),
        check_vma=False,
    )
```

```python
import functools
import jax
import jax.numpy as jnp
from jax import lax
from jax.experimental import pallas as pl
from jax.experimental.pallas import tpu as pltpu
from jax.sharding import PartitionSpec as P
import math

RADIUS = 24
CLIP_LIMIT = 0.08
LOW = math.exp(-CLIP_LIMIT)
HIGH = math.exp(CLIP_LIMIT)
MIB = 1 << 20
STEP = 4
EDGE_STEP = 4
DEEP = 4
GRANT = 20
FIRST = 56


def blur_weights(out_index, in_index, extent, axis):
    spread = RADIUS / 3.0
    distance = (out_index - in_index).astype(jnp.float32)
    inside = (jnp.abs(out_index - in_index) <= RADIUS) & (in_index >= 0) & (in_index < extent)
    kernel = jnp.where(inside, jnp.exp(-distance * distance / (2.0 * spread * spread)), 0.0)
    return kernel / jnp.sum(kernel, axis=axis, keepdims=True)


def numbered(rows, cols):
    return lax.broadcasted_iota(jnp.int32, (rows, cols), 0), lax.broadcasted_iota(jnp.int32, (rows, cols), 1)


def fill_weights(rows, mid_weight, edge_weight, col_high, col_low):
    def put(ref, weights):
        count = weights.shape[0]
        ref[:count], ref[count:] = halves(weights)

    base = lax.axis_index("tile") * rows
    extent = lax.axis_size("tile") * rows
    row, col = numbered(rows - 2 * RADIUS, rows)
    put(mid_weight, blur_weights(base + RADIUS + row, base + col, extent, 1))
    row, col = numbered(2 * RADIUS, 6 * RADIUS)
    row = jnp.where(row < RADIUS, row, row + (rows - 2 * RADIUS))
    col = jnp.where(col < 3 * RADIUS, col, col + (rows - 4 * RADIUS))
    put(edge_weight, blur_weights(base + row, base - RADIUS + col, extent, 1))
    row, col = numbered(*col_high.shape)
    col_high[...], col_low[...] = halves(blur_weights(col, row, col_high.shape[0], 0))


def halves(value):
    high = value.astype(jnp.bfloat16)
    return high, (value - high.astype(jnp.float32)).astype(jnp.bfloat16)


def mul(left, right):
    return jnp.dot(left, right, preferred_element_type=jnp.float32)


def row_blur(high, low, weight):
    rows = weight.shape[0] // 2
    both = mul(weight[...], high)
    return both[:rows] + (both[rows:] + mul(weight[:rows], low))


def column_blur(value, weight_high, weight_low):
    high, low = halves(value)
    return mul(high, weight_high) + (mul(high, weight_low) + mul(low, weight_high))


def retreat(blurred, levelled, fresh, later, factor, put):
    after, running = later[...], factor[...]
    for plane in reversed(range(len(blurred))):
        now = blurred[plane]
        inverse = jnp.clip(after / now, LOW, HIGH)
        if plane == len(blurred) - 1 and fresh is not None:
            inverse = jnp.where(fresh, 1.0, inverse)
        running = running * inverse
        put(plane, levelled[plane] * running)
        after = now
    later[...] = after
    factor[...] = running


def blur_planes(parts, col_high, col_low):
    rows = parts[0].shape[0]
    blurred = column_blur(jnp.concatenate(parts, axis=0), col_high[...], col_low[...])
    return [blurred[plane * rows:(plane + 1) * rows] for plane in range(len(parts))]


def halo_kernel(lower, volume, flat, out, shade, sems):
    rows = flat.shape[0]
    start = jnp.where(lax.axis_index("tile") % 2 == lower, rows - RADIUS, 0)
    at = pl.ds(pl.multiple_of(start, RADIUS), RADIUS)
    copies = [pltpu.make_async_copy(flat.at[at], shade, sems.at[0]), pltpu.make_async_copy(volume.at[:, at], out, sems.at[1])]
    for copy in copies:
        copy.start()
    for copy in copies:
        copy.wait()
    inverse = 1.0 / shade[...]
    for plane in range(out.shape[0]):
        out[plane] = out[plane] * inverse


def middle_step(volume, inverse, row_weight, col_high, col_low, begin):
    rows = volume.shape[1]
    values, parts = [], []
    for plane in range(STEP):
        value = volume[begin + plane] * inverse[...]
        high, low = halves(value)
        parts.append(row_blur(high, low, row_weight))
        values.append(value[RADIUS:rows - RADIUS])
    return values, blur_planes(parts, col_high, col_low)


def deep_kernel(volume, flat, inverse, mid_weight, edge_weight, col_high, col_low, out, deepest, later, factor):
    planes, rows, _ = volume.shape
    fill_weights(rows, mid_weight, edge_weight, col_high, col_low)
    inverse[...] = 1.0 / flat[...]
    later[...] = jnp.ones_like(later)
    factor[...] = jnp.ones_like(factor)
    begin = planes - out.shape[0]
    for at in reversed(range(0, out.shape[0], STEP)):
        values, blurred = middle_step(volume, inverse, mid_weight, col_high, col_low, begin + at)
        fresh = at + STEP == out.shape[0]
        if fresh:
            deepest[...] = blurred[-1]

        def put(plane, value):
            out[at + plane] = value

        retreat(blurred, values, True if fresh else None, later, factor, put)


def middle_steps(volume, inverse, row_weight, col_high, col_low, out, later, factor):
    steps = out.shape[0] // STEP

    def one(index, _):
        at = (steps - 1 - index) * STEP
        values, blurred = middle_step(volume, inverse, row_weight, col_high, col_low, at)

        def put(plane, value):
            out[at + plane] = value

        retreat(blurred, values, None, later, factor, put)
        return 0

    lax.fori_loop(0, steps, one, 0)


def edge_steps(volume, inverse, outer, inner, row_weight, col_high, col_low, out, later, factor, begin, fresh, deepest):
    near = 2 * RADIUS
    rows = volume.shape[1]
    steps = out.shape[0] // EDGE_STEP
    odd = lax.axis_index("tile") % 2 == 1

    def one(index, _):
        at = (steps - 1 - index) * EDGE_STEP
        values, parts = [], []
        for plane in range(EDGE_STEP):
            here = begin + at + plane
            upper = volume[here, :near] * inverse[:near]
            lower = volume[here, rows - near:] * inverse[rows - near:]
            above = jnp.where(odd, inner[here], outer[here])
            below = jnp.where(odd, outer[here], inner[here])
            value = jnp.concatenate([above, upper, lower, below], axis=0)
            high, low = halves(value)
            parts.append(row_blur(high, low, row_weight))
            values.append(jnp.concatenate([upper[:RADIUS], lower[RADIUS:]], axis=0))
        blurred = blur_planes(parts, col_high, col_low)
        start = index == 0 if fresh else None
        if fresh:

            @pl.when(start)
            def _():
                deepest[...] = blurred[-1]

        def put(plane, value):
            out[at + plane] = value

        retreat(blurred, values, start, later, factor, put)
        return 0

    lax.fori_loop(0, steps, one, 0)


def edge_kernel(volume, inverse, outer, inner, row_weight, col_high, col_low, out, deepest, later, factor):
    later[...] = jnp.ones_like(later)
    factor[...] = jnp.ones_like(factor)
    begin = volume.shape[0] - out.shape[0]
    edge_steps(volume, inverse, outer, inner, row_weight, col_high, col_low, out, later, factor, begin, True, deepest)


def shallow_kernel(
    volume, inverse, outer, inner, mid_weight, edge_weight, col_high, col_low, later_mid, factor_mid, later_edge, factor_edge,
    mid_out, mid_later, mid_factor, edge_out, edge_later, edge_factor,
):
    mid_later[...] = later_mid[...]
    mid_factor[...] = factor_mid[...]
    edge_later[...] = later_edge[...]
    edge_factor[...] = factor_edge[...]
    edge_steps(volume, inverse, outer, inner, edge_weight, col_high, col_low, edge_out, edge_later, edge_factor, 0, False, None)
    middle_steps(volume, inverse, mid_weight, col_high, col_low, mid_out, mid_later, mid_factor)


def join_kernel(before_mid, before_edge, first_mid, first_edge, factor_mid, factor_edge, pieces):
    inner, cols = before_mid.shape
    groups = inner // RADIUS + 2
    wide = cols // 4
    for group in range(groups):
        if group in (0, groups - 1):
            at = pl.ds(0 if group == 0 else RADIUS, RADIUS)
            before, first, factor = before_edge[at], first_edge[at], factor_edge[at]
        else:
            at = pl.ds((group - 1) * RADIUS, RADIUS)
            before, first, factor = before_mid[at], first_mid[at], factor_mid[at]
        total = jnp.where(before > 0.0, jnp.clip(before / first, LOW, HIGH), 1.0) / factor
        for part in range(4):
            pieces[group * 4 + part] = total[:, part * wide:(part + 1) * wide]


def scan_kernel(pieces, out):
    running = jnp.ones(pieces.shape[1:], jnp.float32)
    for slab in range(pieces.shape[0]):
        running = running * pieces[slab]
        out[slab] = running


def final_kernel(shallow, deep, shallow_edge, deep_edge, pieces, out, factor, result, sems):
    planes, rows, cols = result.shape
    wide = cols // 4
    rest = shallow.shape[0]
    for group in range(rows // RADIUS):
        for part in range(4):
            factor[group * RADIUS:(group + 1) * RADIUS, part * wide:(part + 1) * wide] = pieces[group * 4 + part]
    copies = []
    for plane in range(planes):
        middle, edge, at = (shallow, shallow_edge, plane) if plane < rest else (deep, deep_edge, plane - rest)
        result[plane, :RADIUS] = edge[at, :RADIUS] * factor[:RADIUS]
        result[plane, RADIUS:rows - RADIUS] = middle[at] * factor[RADIUS:rows - RADIUS]
        result[plane, rows - RADIUS:] = edge[at, RADIUS:] * factor[rows - RADIUS:]
        copy = pltpu.make_async_copy(result.at[plane], out.at[plane], sems.at[plane])
        copy.start()
        copies.append(copy)
    for copy in copies:
        copy.wait()


def shape(*dims):
    return jax.ShapeDtypeStruct(dims, jnp.float32)


def params(mib):
    return pltpu.CompilerParams(vmem_limit_bytes=mib * MIB)


def cost(flops, moved):
    return pl.CostEstimate(flops=int(flops), bytes_accessed=int(moved), transcendentals=0)


def vmem_call(kernel, inputs, outputs, given):
    vmem = pl.BlockSpec(memory_space=pltpu.VMEM)
    return pl.pallas_call(
        kernel,
        in_specs=[vmem] * inputs,
        out_specs=[vmem] * len(outputs),
        out_shape=outputs,
        compiler_params=params(GRANT),
        cost_estimate=given,
    )


def halo_call(volume, flat, lower):
    planes, rows, cols = volume.shape
    return pl.pallas_call(
        functools.partial(halo_kernel, lower),
        in_specs=[pl.BlockSpec(memory_space=pl.ANY)] * 2,
        out_specs=pl.BlockSpec(memory_space=pltpu.VMEM),
        out_shape=shape(planes, RADIUS, cols),
        scratch_shapes=[pltpu.VMEM((RADIUS, cols), jnp.float32), pltpu.SemaphoreType.DMA((2,))],
        compiler_params=params(FIRST),
        cost_estimate=cost(1e6, 2e6),
    )(volume, flat)


def deep_call(volume, flat):
    planes, rows, cols = volume.shape
    inner, near = rows - 2 * RADIUS, 2 * RADIUS
    weights = [(2 * inner, rows), (2 * near, 3 * near), (cols, cols), (cols, cols)]
    outputs = [shape(rows, cols)]
    outputs += [jax.ShapeDtypeStruct(dims, jnp.bfloat16) for dims in weights]
    outputs += [shape(DEEP, inner, cols)] + [shape(inner, cols)] * 3
    return vmem_call(deep_kernel, 2, outputs, cost(6e9, 7e6))(volume, flat)


def final_call(shallow, deep, shallow_edge, deep_edge, pieces):
    _, inner, cols = deep.shape
    planes, rows = shallow.shape[0] + deep.shape[0], inner + 2 * RADIUS
    return pl.pallas_call(
        final_kernel,
        in_specs=[pl.BlockSpec(memory_space=pltpu.VMEM)] * 5,
        out_specs=pl.BlockSpec(memory_space=pl.ANY),
        out_shape=shape(planes, rows, cols),
        scratch_shapes=[
            pltpu.VMEM((rows, cols), jnp.float32),
            pltpu.VMEM((planes, rows, cols), jnp.float32),
            pltpu.SemaphoreType.DMA((planes,)),
        ],
        compiler_params=params(GRANT),
    )(shallow, deep, shallow_edge, deep_edge, pieces)


def swapped(begin, count):
    return [pair for i in range(begin, count - 1, 2) for pair in ((i, i + 1), (i + 1, i))]


def body(volume, flat_field):
    planes, rows, cols = volume.shape
    tiles, slabs = lax.axis_size("tile"), lax.axis_size("depth")
    onward = [(i, i + 1) for i in range(slabs - 1)]
    inner, near, rest = rows - 2 * RADIUS, 2 * RADIUS, planes - DEEP
    outer = lax.ppermute(halo_call(volume, flat_field, 1), "tile", swapped(1, tiles))
    inner_halo = lax.ppermute(halo_call(volume, flat_field, 0), "tile", swapped(0, tiles))
    inverse, mid_weight, edge_weight, col_high, col_low, deep, deepest, later, factor = deep_call(volume, flat_field)
    before_mid = lax.ppermute(deepest, "depth", onward)
    deep_edge, deepest_edge, later_edge, factor_edge = vmem_call(
        edge_kernel, 7, [shape(DEEP, near, cols)] + [shape(near, cols)] * 3, cost(2e9, 4e6)
    )(volume, inverse, outer, inner_halo, edge_weight, col_high, col_low)
    before_edge = lax.ppermute(deepest_edge, "depth", onward)
    outputs = [shape(rest, inner, cols)] + [shape(inner, cols)] * 2 + [shape(rest, near, cols)] + [shape(near, cols)] * 2
    shallow, first_mid, factor_mid, shallow_edge, first_edge, factor_edge = vmem_call(shallow_kernel, 12, outputs, cost(8e9, 1e7))(
        volume, inverse, outer, inner_halo, mid_weight, edge_weight, col_high, col_low, later, factor, later_edge, factor_edge
    )
    traded = shape(slabs, RADIUS, cols // 4)
    (pieces,) = vmem_call(join_kernel, 6, [traded], cost(1e6, 2e6))(
        before_mid, before_edge, first_mid, first_edge, factor_mid, factor_edge
    )
    mine = lax.all_to_all(pieces, "depth", 0, 0, tiled=True)
    (reached,) = vmem_call(scan_kernel, 1, [traded], cost(1e6, 1e6))(mine)
    back = lax.all_to_all(reached, "depth", 0, 0, tiled=True)
    return final_call(shallow, deep, shallow_edge, deep_edge, back)


def solution(mesh):
    return jax.shard_map(
        body,
        mesh=mesh,
        in_specs=(P("depth", "tile", None), P("tile", None)),
        out_specs=P("depth", "tile", None),
        check_vma=False,
    )
```
